32 devices in a mesh: groups: 2 (over x), patch: 16 (over z, y, core).
Axes of the slice: x: 2, y: 2, z: 4, core: 2. Of those that a mesh axis runs over, the one named last changes fastest.
Arguments:
- nodes: bfloat16 [8192, 512], P(('groups', 'patch')), parts along dimension 0, may hold values from -6 to 6
- edges: bfloat16 [65536, 512], P(('groups', 'patch')), parts along dimension 0, may hold values from -6 to 6
- cot_nodes: bfloat16 [8192, 512], P(('groups', 'patch')), parts along dimension 0, may hold values from -6 to 6
- w_edge_in: bfloat16 [1536, 512], replicated, may hold values from -0.15625 to 0.15625
- w_edge_out: bfloat16 [512, 512], replicated, may hold values from -0.25 to 0.25
- w_node_in: bfloat16 [1024, 512], replicated, may hold values from -0.1875 to 0.1875
- w_node_out: bfloat16 [512, 512], replicated, may hold values from -0.25 to 0.25
- send_rows: int32 [32, 16, 4], P(('groups', 'patch')), parts along dimension 0, may hold values from 0 to 255
- edge_sender: int32 [65536], P(('groups', 'patch')), parts along dimension 0, may hold values from 0 to 319
- edge_receiver: int32 [65536], P(('groups', 'patch')), parts along dimension 0, may hold values from -1 to 255, as said below
Outputs:
- grad_nodes: bfloat16 [8192, 512], P(('groups', 'patch')), parts along dimension 0
- grad_edges: bfloat16 [65536, 512], P(('groups', 'patch')), parts along dimension 0
- grad_edge_in: float32 [3072, 512], P(('groups', 'patch')), parts along dimension 0
- grad_edge_out: float32 [1024, 512], P(('groups', 'patch')), parts along dimension 0
- grad_node_in: float32 [2048, 512], P(('groups', 'patch')), parts along dimension 0
- grad_node_out: float32 [1024, 512], P(('groups', 'patch')), parts along dimension 0
The draws below stay inside these ranges and needn't reach their ends.
There are 2 independent parts, one for each index of `groups`. The reference program is written for one: setup_inputs(seed, part) draws one part's arguments, and reference() takes and returns one part's arrays. A program takes and returns all parts, laid end to end along the dimension named above; an argument that names none is the same for every part. Nothing has to cross between parts.
Inputs may be any that keep to these rules, and one draw needn't show every extreme that they name: `edge_receiver`: on each device the empty slots (-1) come last and are at most half of its 2048 slots; some device has none and some device has exactly half empty.
All inputs are finite; a program needn't handle non-finite values.
Results may differ from the reference program's by a relative error of at most 0.013.
Values may be sent and summed in bfloat16 or wider, within the bound.
No kernel may reach another device: no remote copies, remote signals or barrier semaphores. Data moves between devices by JAX's collectives and lax.ppermute only.
A program may use at most 128 MiB of HBM per device.

```python
import jax
import jax.numpy as jnp
from jax import lax

D = 512
NODE_DEV = 256
EDGE_DEV = 2048
SLOT = 4
NODES = 4096
EDGES = 32768
N_PATCH = 16


def draw_edge_receiver(key, part):
    key = jax.random.fold_in(key, 7)
    first, second, third = jax.random.split(key, 3)
    receivers = jax.random.randint(first, (N_PATCH, EDGE_DEV), 0, NODE_DEV)
    cuts = jax.random.randint(second, (N_PATCH,), 0, EDGE_DEV // 2 + 1)
    fullest = jax.random.randint(third, (), 0, N_PATCH)
    devices = jnp.arange(N_PATCH)
    cuts = jnp.where(devices == fullest, 0, cuts)
    cuts = jnp.where(devices == (fullest + 1) % N_PATCH, EDGE_DEV // 2, cuts)
    live = jnp.arange(EDGE_DEV)[None, :] < (EDGE_DEV - cuts)[:, None]
    return jnp.where(live, receivers, -1).reshape(-1).astype(jnp.int32)


def with_ends(entries, stream_key, least, top_value):
    index_at = [jax.random.randint(jax.random.fold_in(stream_key, axis), (), 0, length) for axis, length in enumerate(entries.shape)]
    widest = entries.shape.index(max(entries.shape))
    beside = index_at[:widest] + [(index_at[widest] + 1) % entries.shape[widest]] + index_at[widest + 1:]
    return entries.at[tuple(index_at)].set(least).at[tuple(beside)].set(top_value)


def level_of(rng, dims, pieces, low, largest):
    factor_of = 1.0
    for position, parts in pieces:
        draws = jax.random.uniform(jax.random.fold_in(jax.random.fold_in(rng, 6), position), (parts,), jnp.float32, low / len(pieces), largest / len(pieces))
        factor_of = factor_of * jnp.repeat(jnp.exp(draws), dims[position] // parts).reshape((-1,) + (1,) * (len(dims) - 1 - position))
    return factor_of


def noise(rng, shape, spread, reach, cuts=(), kind=jnp.bfloat16):
    values = spread * jax.random.normal(rng, shape, jnp.float32)
    if cuts:
        values = values * level_of(rng, shape, cuts, -0.22, 0.18)
    return jnp.clip(values, -reach, reach).astype(kind)


def setup_inputs(seed: int = 0, part: int = 0) -> dict:
    splits = jax.random.split(jax.random.key(seed), 11)
    part_keys = jax.random.split(jax.random.fold_in(splits[10], part), 11)
    return {
        "nodes": noise(part_keys[0], (NODES, D), 1.0, 6.0, ((0, 16),)),
        "edges": noise(part_keys[1], (EDGES, D), 1.0, 6.0, ((0, 16),)),
        "cot_nodes": noise(part_keys[2], (NODES, D), 1.0, 6.0, ((0, 16),)),
        "w_edge_in": noise(splits[3], (3 * D, D), (3 * D) ** -0.5, 0.15625),
        "w_edge_out": noise(splits[4], (D, D), D ** -0.5, 0.25),
        "w_node_in": noise(splits[5], (2 * D, D), (2 * D) ** -0.5, 0.1875),
        "w_node_out": noise(splits[6], (D, D), D ** -0.5, 0.25),
        "send_rows": with_ends(jax.random.randint(part_keys[7], (N_PATCH, N_PATCH, SLOT), 0, NODE_DEV), jax.random.fold_in(part_keys[7], 1), 0, NODE_DEV - 1).astype(jnp.int32),
        "edge_sender": with_ends(jax.random.randint(part_keys[8], (EDGES,), 0, NODE_DEV + N_PATCH * SLOT), jax.random.fold_in(part_keys[8], 1), 0, (NODE_DEV + N_PATCH * SLOT) - 1).astype(jnp.int32),
        "edge_receiver": draw_edge_receiver(jax.random.fold_in(jax.random.fold_in(splits[10], part), 71), part),
    }


def normalize(values):
    center = values - lax.optimization_barrier(jnp.mean(values, axis=-1, keepdims=True))
    inv_std = lax.rsqrt(lax.optimization_barrier(jnp.mean(center * center, axis=-1, keepdims=True)) + 1e-05)
    return (center * inv_std, inv_std)

def norm_back(upstream, normed, inv_std):
    return inv_std * (upstream - lax.optimization_barrier(jnp.mean(upstream, axis=-1, keepdims=True)) - normed * lax.optimization_barrier(jnp.mean(upstream * normed, axis=-1, keepdims=True)))

def silu_slope(values):
    sigma = jax.nn.sigmoid(values)
    return sigma * (1.0 + values * (1.0 - sigma))

def exact_dot(left, right):
    return jnp.dot(left, right, precision=lax.Precision.HIGHEST, preferred_element_type=jnp.float32)

def reference(nodes, edges, cot_nodes, w_edge_in, w_edge_out, w_node_in, w_node_out, send_rows, edge_sender, edge_receiver):
    width = D
    device = (jnp.arange(EDGE_DEV * N_PATCH, dtype=jnp.int32) // EDGE_DEV).astype(jnp.int32)
    halo_index = jnp.clip(edge_sender - NODE_DEV, 0, N_PATCH * SLOT - 1).astype(jnp.int32)
    source = (halo_index // SLOT).astype(jnp.int32)
    slot_pos = (halo_index % SLOT).astype(jnp.int32)
    remote = source * NODE_DEV + send_rows[source, device, slot_pos]
    global_send = jnp.where(edge_sender < NODE_DEV, device * NODE_DEV + edge_sender, remote).astype(jnp.int32)
    live = edge_receiver >= 0
    global_recv = (device * NODE_DEV + jnp.maximum(edge_receiver, 0)).astype(jnp.int32)
    total_nodes = NODE_DEV * N_PATCH
    w_self = w_edge_in[:width]
    w_send = w_edge_in[width:2 * width]
    w_recv = w_edge_in[2 * width:]
    w_host = w_node_in[:width]
    w_inbox = w_node_in[width:]
    proj_send = jnp.dot(nodes, w_send, preferred_element_type=jnp.float32).astype(jnp.bfloat16)
    proj_recv = jnp.dot(nodes, w_recv, preferred_element_type=jnp.float32).astype(jnp.bfloat16)
    pre_act = jnp.dot(edges, w_self, preferred_element_type=jnp.float32) + proj_send[global_send].astype(jnp.float32) + proj_recv[global_recv].astype(jnp.float32)
    zeta = jax.nn.silu(pre_act).astype(jnp.bfloat16)
    edge_normed, edge_inv = normalize(jnp.dot(zeta, w_edge_out, preferred_element_type=jnp.float32))
    message = edge_normed.astype(jnp.bfloat16)
    live_message = jnp.where(live[:, None], message.astype(jnp.float32), jnp.float32(0.0))
    inbox = jax.ops.segment_sum(live_message, global_recv, total_nodes).astype(jnp.bfloat16)
    node_pre = jnp.dot(nodes, w_host, preferred_element_type=jnp.float32) + jnp.dot(inbox, w_inbox, preferred_element_type=jnp.float32)
    node_zeta = jax.nn.silu(node_pre).astype(jnp.bfloat16)
    node_normed, node_inv = normalize(jnp.dot(node_zeta, w_node_out, preferred_element_type=jnp.float32))
    upstream = cot_nodes.astype(jnp.float32)
    node_dy = norm_back(upstream, node_normed, node_inv).astype(jnp.bfloat16)
    grad_node_out = jnp.dot(node_zeta.T, node_dy, preferred_element_type=jnp.float32)
    node_db = (jnp.dot(node_dy, w_node_out.T, preferred_element_type=jnp.float32) * silu_slope(node_pre)).astype(jnp.bfloat16)
    grad_node_in = jnp.dot(jnp.concatenate([nodes, inbox], axis=1).T, node_db, preferred_element_type=jnp.float32)
    inbox_grad = jnp.dot(node_db, w_inbox.T, preferred_element_type=jnp.float32).astype(jnp.bfloat16)
    node_grad = upstream + jnp.dot(node_db, w_host.T, preferred_element_type=jnp.float32)
    message_grad = jnp.where(live[:, None], inbox_grad[global_recv].astype(jnp.float32), jnp.float32(0.0))
    edge_dy = norm_back(message_grad, edge_normed, edge_inv).astype(jnp.bfloat16)
    grad_edge_out = jnp.dot(zeta.T, edge_dy, preferred_element_type=jnp.float32)
    edge_da = (jnp.dot(edge_dy, w_edge_out.T, preferred_element_type=jnp.float32) * silu_slope(pre_act)).astype(jnp.bfloat16)
    grad_edges = jnp.dot(edge_da, w_self.T, preferred_element_type=jnp.float32).astype(jnp.bfloat16)
    self_grad = jnp.dot(edges.T, edge_da, preferred_element_type=jnp.float32)
    da_float = edge_da.astype(jnp.float32)
    send_sums = jax.ops.segment_sum(da_float, global_send, total_nodes)
    recv_sums = jax.ops.segment_sum(jnp.where(live[:, None], da_float, jnp.float32(0.0)), global_recv, total_nodes)
    nodes_float = nodes.astype(jnp.float32)
    send_wgrad = exact_dot(nodes_float.T, send_sums)
    recv_wgrad = exact_dot(nodes_float.T, recv_sums)
    node_grad = node_grad + exact_dot(send_sums, w_send.astype(jnp.float32).T) + exact_dot(recv_sums, w_recv.astype(jnp.float32).T)
    grad_edge_in = jnp.concatenate([self_grad, send_wgrad, recv_wgrad], axis=0)
    return (node_grad.astype(jnp.bfloat16), grad_edges, grad_edge_in, grad_edge_out, grad_node_in, grad_node_out)
```

```python
import functools

import jax
import jax.numpy as jnp
from jax import lax
from jax.experimental import pallas as pl
from jax.experimental.pallas import tpu as pltpu
from jax.sharding import PartitionSpec as P

BF16 = jnp.bfloat16
F32 = jnp.float32
EPS = 1e-05
LANES = 128
BLOCK = 256


def mm(left, right):
    return jnp.dot(left, right, preferred_element_type=F32)


def mm_rows(left, right):
    return lax.dot_general(left, right, (((0,), (0,)), ((), ())), preferred_element_type=F32)


def mm_cols(left, right):
    return lax.dot_general(left, right, (((1,), (1,)), ((), ())), preferred_element_type=F32)


def sigmoid(values):
    return 0.5 * jnp.tanh(0.5 * values) + 0.5


def normalize(values):
    center = values - jnp.mean(values, axis=-1, keepdims=True)
    inv_std = lax.rsqrt(jnp.mean(center * center, axis=-1, keepdims=True) + EPS)
    return center * inv_std, inv_std


def norm_back(upstream, normed, inv_std):
    return inv_std * (
        upstream
        - jnp.mean(upstream, axis=-1, keepdims=True)
        - normed * jnp.mean(upstream * normed, axis=-1, keepdims=True)
    )


def cube_masks(count):
    bits = count.bit_length() - 1
    masks = [1 << i for i in range(bits)]
    if bits >= 3:
        masks[-1] |= masks[-2]
    return masks


def cube_orders(count):
    rest = list(range(1, count.bit_length() - 1))
    return [0] + rest, [0] + rest[1:] + rest[:1]


def cube_position(target, me, count):
    bits = count.bit_length() - 1
    apart = target ^ me
    coords = [(apart >> i) & 1 for i in range(bits)]
    if bits >= 3:
        coords[-2] = coords[-2] ^ coords[-1]
    even, odd = [sum(coords[dim] << (bits - 1 - j) for j, dim in enumerate(order)) for order in cube_orders(count)]
    return jnp.where((target & 1) == 0, even, odd)


def cube_reduce(blocks, count):
    masks, orders = cube_masks(count), cube_orders(count)
    for step in range(count.bit_length() - 1):
        half = blocks.shape[0] // 2
        pairs = [(i, i ^ masks[orders[i & 1][step]]) for i in range(count)]
        arrived = lax.ppermute(blocks[half:], "patch", pairs)
        total = blocks[:half].astype(F32) + arrived.astype(F32)
        blocks = total if half == 1 else total.astype(BF16)
    return blocks[0]


def one_hot_cols(ids, width):
    rows = ids.shape[1]
    spread = jnp.transpose(jnp.broadcast_to(ids, (LANES, rows)))
    lane = lax.broadcasted_iota(jnp.int32, (rows, LANES), 1)
    tiles = [jnp.where(spread == lane + start, 1.0, 0.0).astype(BF16) for start in range(0, width, LANES)]
    return jnp.concatenate(tiles, axis=1)[:, :width]


def hot_cols(first, second, width):
    rows = first.shape[1]
    left = jnp.transpose(jnp.broadcast_to(first, (LANES, rows)))
    right = jnp.transpose(jnp.broadcast_to(second, (LANES, rows)))
    lane = lax.broadcasted_iota(jnp.int32, (rows, LANES), 1)
    tiles = [
        jnp.where((left == lane + start) | (right == lane + start), 1.0, 0.0).astype(BF16)
        for start in range(0, width, LANES)
    ]
    return jnp.concatenate(tiles, axis=1)


def hot_rows(first, second, width):
    row = lax.broadcasted_iota(jnp.int32, (width, first.shape[1]), 0)
    return jnp.where((row == first) | (row == second), 1.0, 0.0).astype(BF16)


def layer_kernel(
    count,
    me_ref,
    nodes_ref,
    halo_ref,
    edges_ref,
    cot_ref,
    w_edge_in_ref,
    w_edge_out_ref,
    w_node_in_ref,
    w_node_out_ref,
    send_ref,
    recv_ref,
    blocks_ref,
    da_ref,
    sums_ref,
    node_part_ref,
    table,
    zeta,
    slope,
    normed,
    inv,
    agg,
    dagg,
    grads_no,
    grads_ni,
    grads_eo,
    grads_ei,
):
    owned, width = nodes_ref.shape
    n_halo = halo_ref.shape[0]
    n_edges = edges_ref.shape[0]
    n_table = table.shape[0]
    n_blocks = n_edges // BLOCK
    w_self = w_edge_in_ref.at[:width]
    w_send = w_edge_in_ref.at[width : 2 * width]
    w_recv = w_edge_in_ref.at[2 * width :]
    w_host = w_node_in_ref.at[:width]
    w_inbox = w_node_in_ref.at[width:]

    table[:owned] = mm(nodes_ref[...], w_send[...]).astype(BF16)
    table[owned : 2 * owned] = mm(nodes_ref[...], w_recv[...]).astype(BF16)
    table[2 * owned : 2 * owned + n_halo] = mm(halo_ref[...], w_send[...]).astype(BF16)
    if n_table > 2 * owned + n_halo:
        table[2 * owned + n_halo :] = jnp.zeros((n_table - 2 * owned - n_halo, width), BF16)
    agg[...] = jnp.zeros_like(agg)

    def ids(block):
        cols = pl.ds(pl.multiple_of(block * BLOCK, BLOCK), BLOCK)
        sender = send_ref[:, cols]
        receiver = recv_ref[:, cols]
        sender = jnp.where(sender < owned, sender, sender + owned)
        return sender, jnp.maximum(receiver, 0) + owned, receiver

    @pl.loop(0, n_blocks)
    def _(block):
        rows = pl.ds(pl.multiple_of(block * BLOCK, BLOCK), BLOCK)
        sender, safe, receiver = ids(block)
        pre = mm(edges_ref[rows], w_self[...]) + mm(hot_cols(sender, safe, n_table), table[...])
        sigma = sigmoid(pre)
        zed = (pre * sigma).astype(BF16)
        zeta[rows] = zed
        slope[rows] = (sigma * (1.0 + pre * (1.0 - sigma))).astype(BF16)
        unit, inv_std = normalize(mm(zed, w_edge_out_ref[...]))
        message = unit.astype(BF16)
        normed[rows] = message
        inv[rows] = inv_std
        agg[...] += mm(hot_rows(receiver, receiver, owned), message)

    inbox = agg[...].astype(BF16)
    nodes = nodes_ref[...]
    pre = mm(nodes, w_host[...]) + mm(inbox, w_inbox[...])
    sigma = sigmoid(pre)
    zed = (pre * sigma).astype(BF16)
    unit, inv_std = normalize(mm(zed, w_node_out_ref[...]))
    upstream = cot_ref[...].astype(F32)
    dy = norm_back(upstream, unit, inv_std).astype(BF16)
    db = (mm_cols(dy, w_node_out_ref[...]) * (sigma * (1.0 + pre * (1.0 - sigma)))).astype(BF16)
    dagg[...] = mm_cols(db, w_inbox[...]).astype(BF16)
    node_part_ref[...] = upstream + mm_cols(db, w_host[...])
    grads_no[...] = mm_rows(zed, dy)
    grads_ni[:width] = mm_rows(nodes, db)
    grads_ni[width:] = mm_rows(inbox, db)

    sums_ref[...] = jnp.zeros_like(sums_ref)
    grads_eo[...] = jnp.zeros_like(grads_eo)
    grads_ei[:width] = jnp.zeros((width, width), F32)

    @pl.loop(0, n_blocks)
    def _(block):
        rows = pl.ds(pl.multiple_of(block * BLOCK, BLOCK), BLOCK)
        sender, safe, receiver = ids(block)
        up = mm(one_hot_cols(receiver, owned), dagg[...])
        dye = norm_back(up, normed[rows].astype(F32), inv[rows]).astype(BF16)
        grads_eo[...] += mm_rows(zeta[rows], dye)
        da = (mm_cols(dye, w_edge_out_ref[...]) * slope[rows].astype(F32)).astype(BF16)
        da_ref[rows] = da
        grads_ei[:width] += mm_rows(edges_ref[rows], da)
        sums_ref[...] += mm(hot_rows(sender, safe, n_table), da)

    own = sums_ref[:owned].astype(BF16)
    far = sums_ref[2 * owned : 2 * owned + n_halo].astype(BF16)
    grads_ei[width : 2 * width] = mm_rows(nodes, own) + mm_rows(halo_ref[...], far)
    grads_ei[2 * width :] = mm_rows(nodes, sums_ref[owned : 2 * owned].astype(BF16))

    me = me_ref[0]
    sources = (grads_no, grads_ni, grads_eo, grads_ei)
    shares = [source.shape[0] // count for source in sources]
    spare = blocks_ref.shape[1] - sum(shares)

    @pl.loop(0, count)
    def _(target):
        parts = [
            source[pl.ds(pl.multiple_of(target * share, share), share)] for source, share in zip(sources, shares)
        ]
        if spare:
            parts.append(jnp.zeros((spare, width), F32))
        blocks_ref[cube_position(target, me, count)] = jnp.concatenate(parts, axis=0).astype(BF16)


def layer(count, me, nodes, halo, edges, cot, w_edge_in, w_edge_out, w_node_in, w_node_out, sender, receiver):
    owned, width = nodes.shape
    n_edges = edges.shape[0]
    n_table = -(-(2 * owned + halo.shape[0]) // LANES) * LANES
    share = sum(r * width // count for r in (1, 2, 1, 3))
    share = -(-share // 16) * 16
    vmem = pl.BlockSpec(memory_space=pltpu.VMEM)
    smem = pl.BlockSpec(memory_space=pltpu.SMEM)
    return pl.pallas_call(
        functools.partial(layer_kernel, count),
        out_shape=(
            jax.ShapeDtypeStruct((count, share, width), BF16),
            jax.ShapeDtypeStruct((n_edges, width), BF16),
            jax.ShapeDtypeStruct((n_table, width), F32),
            jax.ShapeDtypeStruct((owned, width), F32),
        ),
        in_specs=[smem] + [vmem] * 10,
        out_specs=(vmem,) * 4,
        scratch_shapes=[
            pltpu.VMEM((n_table, width), BF16),
            pltpu.VMEM((n_edges, width), BF16),
            pltpu.VMEM((n_edges, width), BF16),
            pltpu.VMEM((n_edges, width), BF16),
            pltpu.VMEM((n_edges, 1), F32),
            pltpu.VMEM((owned, width), F32),
            pltpu.VMEM((owned, width), BF16),
            pltpu.VMEM((width, width), F32),
            pltpu.VMEM((2 * width, width), F32),
            pltpu.VMEM((width, width), F32),
            pltpu.VMEM((3 * width, width), F32),
        ],
        compiler_params=pltpu.CompilerParams(vmem_limit_bytes=56 << 20),
        name="layer",
    )(me, nodes, halo, edges, cot, w_edge_in, w_edge_out, w_node_in, w_node_out, sender, receiver)


def trade(rows):
    return lax.all_to_all(rows, "patch", split_axis=0, concat_axis=0, tiled=True)


def body(
    count,
    nodes,
    edges,
    cot_nodes,
    w_edge_in,
    w_edge_out,
    w_node_in,
    w_node_out,
    send_rows,
    edge_sender,
    edge_receiver,
):
    owned, width = nodes.shape
    flat = send_rows.reshape(-1)
    pick = (flat[:, None] == jnp.arange(owned, dtype=jnp.int32)[None, :]).astype(BF16)
    halo = trade(mm(pick, nodes).astype(BF16))
    me = lax.axis_index("patch").astype(jnp.int32).reshape(1)
    blocks, edge_da, sums, node_part = layer(
        count,
        me,
        nodes,
        halo,
        edges,
        cot_nodes,
        w_edge_in,
        w_edge_out,
        w_node_in,
        w_node_out,
        edge_sender.reshape(1, -1),
        edge_receiver.reshape(1, -1),
    )
    total = cube_reduce(blocks, count)
    returned = trade(sums[2 * owned : 2 * owned + flat.size].astype(BF16))
    edge_grad = mm_cols(edge_da, w_edge_in[:width]).astype(BF16)
    own_sums = (sums[:owned] + mm_rows(pick, returned)).astype(BF16)
    node_grad = (
        node_part
        + mm_cols(own_sums, w_edge_in[width : 2 * width])
        + mm_cols(sums[owned : 2 * owned].astype(BF16), w_edge_in[2 * width :])
    ).astype(BF16)
    cuts = [width // count * part for part in (1, 3, 4, 7)]
    return (
        node_grad,
        edge_grad,
        total[cuts[2] : cuts[3]],
        total[cuts[1] : cuts[2]],
        total[cuts[0] : cuts[1]],
        total[: cuts[0]],
    )


def solution(mesh):
    rows = P(("groups", "patch"), None)
    flat = P(("groups", "patch"))
    return jax.shard_map(
        functools.partial(body, mesh.shape["patch"]),
        mesh=mesh,
        in_specs=(rows, rows, rows, P(), P(), P(), P(), P(("groups", "patch"), None, None), flat, flat),
        out_specs=(rows,) * 6,
        check_vma=False,
    )
```

```python
import functools

import jax
import jax.numpy as jnp
from jax import lax
from jax.experimental import pallas as pl
from jax.experimental.pallas import tpu as pltpu
from jax.sharding import PartitionSpec as P

BF16 = jnp.bfloat16
F32 = jnp.float32
EPS = 1e-05
LANES = 128
BLOCK = 1024
TILE = 256
HALO_ROWS = 8
GRID_BLOCK = 1024


def mm(left, right):
    return jnp.dot(left, right, preferred_element_type=F32)


def mm_rows(left, right):
    return lax.dot_general(left, right, (((0,), (0,)), ((), ())), preferred_element_type=F32)


def mm_cols(left, right):
    return lax.dot_general(left, right, (((1,), (1,)), ((), ())), preferred_element_type=F32)


def sigmoid(values):
    return 0.5 * jnp.tanh(0.5 * values) + 0.5


def normalize(values):
    center = values - jnp.mean(values, axis=-1, keepdims=True)
    inv_std = lax.rsqrt(jnp.mean(center * center, axis=-1, keepdims=True) + EPS)
    return center * inv_std, inv_std


def norm_back(upstream, normed, inv_std):
    return inv_std * (
        upstream
        - jnp.mean(upstream, axis=-1, keepdims=True)
        - normed * jnp.mean(upstream * normed, axis=-1, keepdims=True)
    )


def cube_masks(count):
    return [1 << i for i in range(count.bit_length() - 1)]


def cube_orders(count):
    rest = list(range(1, count.bit_length() - 1))
    return [0] + rest, [0] + rest[:2][::-1] + rest[2:]


def cube_place(apart, parity, count):
    bits = count.bit_length() - 1
    coords = [(apart >> i) & 1 for i in range(bits)]
    even, odd = [sum(coords[dim] << (bits - 1 - j) for j, dim in enumerate(order)) for order in cube_orders(count)]
    return jnp.where(parity == 0, even, odd)


def cube_permute(blocks, step, count):
    mask, orders = cube_masks(count), cube_orders(count)
    pairs = [(i, i ^ mask[orders[i & 1][step]]) for i in range(count)]
    return lax.ppermute(blocks, "patch", pairs)


def one_hot_cols(ids, width):
    rows = ids.shape[1]
    spread = jnp.transpose(jnp.broadcast_to(ids, (LANES, rows)))
    lane = lax.broadcasted_iota(jnp.int32, (rows, LANES), 1)
    tiles = [jnp.where(spread == lane + start, 1.0, 0.0).astype(BF16) for start in range(0, width, LANES)]
    return jnp.concatenate(tiles, axis=1)[:, :width]


def hot_cols(first, second, width):
    rows = first.shape[1]
    left = jnp.transpose(jnp.broadcast_to(first, (LANES, rows)))
    right = jnp.transpose(jnp.broadcast_to(second, (LANES, rows)))
    lane = lax.broadcasted_iota(jnp.int32, (rows, LANES), 1)
    tiles = [
        jnp.where((left == lane + start) | (right == lane + start), 1.0, 0.0).astype(BF16)
        for start in range(0, width, LANES)
    ]
    return jnp.concatenate(tiles, axis=1)


def hot_rows(first, second, width):
    row = lax.broadcasted_iota(jnp.int32, (width, first.shape[1]), 0)
    return jnp.where((row == first) | (row == second), 1.0, 0.0).astype(BF16)


def edge_ids(rows, owned, slot, send_ref, recv_ref, block_of):
    sender = send_ref[:, rows]
    receiver = recv_ref[:, rows]
    far = sender - owned
    sender = jnp.where(far < 0, sender, 2 * owned + block_of(far // slot) + far % slot)
    return sender, jnp.maximum(receiver, 0) + owned, receiver


def take_rows(step, count, slot):
    weight = count >> (step + 1)
    shape = (count // 2 * slot, count * slot)
    out = lax.broadcasted_iota(jnp.int32, shape, 0)
    block, row = out // slot, out % slot
    place = block // weight * 2 * weight + weight + block % weight
    return jnp.where(lax.broadcasted_iota(jnp.int32, shape, 1) == place * slot + row, 1.0, 0.0).astype(BF16)


def put_blocks(sources, me, count, keep_ref, send_ref):
    shares = [source.shape[0] // count for source in sources]
    half = count // 2
    size = keep_ref.shape[0] // half
    spare = size - sum(shares)

    @pl.loop(0, count)
    def _(target):
        parts = [
            source[pl.ds(pl.multiple_of(target * share, share), share)] for source, share in zip(sources, shares)
        ]
        if spare:
            parts.append(jnp.zeros((spare, keep_ref.shape[1]), F32))
        block = jnp.concatenate(parts, axis=0).astype(BF16)
        place = cube_place(target ^ me, target & 1, count)

        @pl.when(place < half)
        def _():
            keep_ref[pl.ds(pl.multiple_of(place * size, size), size)] = block

        @pl.when(place >= half)
        def _():
            send_ref[pl.ds(pl.multiple_of((place - half) * size, size), size)] = block


def pick_kernel(count, me_ref, picks_ref, nodes_ref, pick_ref, rows_ref):
    slot = picks_ref.shape[0]
    owned = nodes_ref.shape[0]
    me = me_ref[0]

    def choose(rows, start):
        shape = (rows, count)
        row = lax.broadcasted_iota(jnp.int32, shape, 0)
        first = start(lax.broadcasted_iota(jnp.int32, shape, 1))
        ids = jnp.zeros(shape, jnp.int32)
        for place in range(slot):
            ids = ids + jnp.where(row == first + place, picks_ref[place : place + 1] + 1, 0)
        ids = jnp.sum(ids.astype(F32), axis=1, keepdims=True).astype(jnp.int32) - 1
        node = lax.broadcasted_iota(jnp.int32, (rows, owned), 1)
        return jnp.where(node == ids, 1.0, 0.0).astype(BF16)

    rows_ref[...] = mm(choose(count * HALO_ROWS, lambda device: device * HALO_ROWS), nodes_ref[...]).astype(BF16)
    pick_ref[...] = choose(count * slot, lambda device: cube_place(device ^ me, me & 1, count) * slot)


def local_kernel(send_ref, recv_ref, nodes_ref, w_edge_in_ref, edges_ref, base_ref, table):
    owned, width = nodes_ref.shape

    @pl.when(pl.program_id(0) == 0)
    def _():
        nodes = nodes_ref[...]
        table[:owned] = mm(nodes, w_edge_in_ref[width : 2 * width]).astype(BF16)
        table[owned:] = mm(nodes, w_edge_in_ref[2 * width :]).astype(BF16)

    sender = send_ref[...]
    sender = jnp.where(sender < owned, sender, -1)
    hot = hot_cols(sender, jnp.maximum(recv_ref[...], 0) + owned, 2 * owned)
    base_ref[...] = mm(edges_ref[...], w_edge_in_ref[:width]) + mm(hot, table[...])


def forward_kernel(
    count,
    slot,
    me_ref,
    send_ref,
    recv_ref,
    halo_ref,
    w_edge_in_far,
    base_far,
    w_edge_out_far,
    nodes_far,
    w_node_in_far,
    w_node_out_far,
    cot_far,
    edges_far,
    keep_ref,
    away_ref,
    zeta_ref,
    slope_ref,
    normed_ref,
    inv_ref,
    dagg_ref,
    node_part_ref,
    nodes_ref,
    w_edge_out_ref,
    edges_ref,
    w_send,
    w_recv,
    base,
    w_node_in_ref,
    w_node_out_ref,
    cot_ref,
    table,
    agg,
    grads_no,
    grads_ni,
    base_sems,
    sems,
):
    owned, width = nodes_ref.shape
    n_table = table.shape[0]
    n_blocks = base.shape[0] // BLOCK

    def block_rows(block):
        return pl.ds(pl.multiple_of(block * BLOCK, BLOCK), BLOCK)

    def base_copy(block):
        rows = block_rows(block)
        return pltpu.make_async_copy(base_far.at[rows], base.at[rows], base_sems.at[block])

    pairs = (
        (w_edge_in_far.at[width : 2 * width], w_send),
        (w_edge_out_far, w_edge_out_ref),
        (nodes_far, nodes_ref),
        (w_node_in_far, w_node_in_ref),
        (w_node_out_far, w_node_out_ref),
        (cot_far, cot_ref),
        (edges_far, edges_ref),
        (w_edge_in_far.at[2 * width :], w_recv),
    )
    copies = [pltpu.make_async_copy(src, dst, sems.at[i]) for i, (src, dst) in enumerate(pairs)]
    copies[0].start()
    base_copy(0).start()
    copies[1].start()

    @pl.loop(1, n_blocks)
    def _(block):
        base_copy(block).start()

    for copy in copies[2:]:
        copy.start()
    agg[...] = jnp.zeros_like(agg)
    copies[0].wait()
    table[...] = mm(halo_ref[...], w_send[...]).astype(BF16)
    copies[1].wait()

    @pl.loop(0, n_blocks)
    def _(block):
        rows = block_rows(block)
        base_copy(block).wait()
        sender, _, receiver = edge_ids(rows, owned, slot, send_ref, recv_ref, lambda device: device * HALO_ROWS)
        pre = base[rows] + mm(one_hot_cols(sender - 2 * owned, n_table), table[...])
        sigma = sigmoid(pre)
        zed = (pre * sigma).astype(BF16)
        zeta_ref[rows] = zed
        slope_ref[rows] = (sigma * (1.0 + pre * (1.0 - sigma))).astype(BF16)
        unit, inv_std = normalize(mm(zed, w_edge_out_ref[...]))
        message = unit.astype(BF16)
        normed_ref[rows] = message
        inv_ref[rows] = inv_std
        agg[...] += mm(hot_rows(receiver, receiver, owned), message)

    for copy in copies[2:]:
        copy.wait()
    nodes = nodes_ref[...]
    inbox = agg[...].astype(BF16)
    pre = mm(nodes, w_node_in_ref[:width]) + mm(inbox, w_node_in_ref[width:])
    sigma = sigmoid(pre)
    zed = (pre * sigma).astype(BF16)
    unit, inv_std = normalize(mm(zed, w_node_out_ref[...]))
    upstream = cot_ref[...].astype(F32)
    dy = norm_back(upstream, unit, inv_std).astype(BF16)
    db = (mm_cols(dy, w_node_out_ref[...]) * (sigma * (1.0 + pre * (1.0 - sigma)))).astype(BF16)
    dagg_ref[...] = mm_cols(db, w_node_in_ref[width:]).astype(BF16)
    node_part_ref[...] = upstream + mm_cols(db, w_node_in_ref[:width])
    grads_no[...] = mm_rows(zed, dy)
    grads_ni[:width] = mm_rows(nodes, db)
    grads_ni[width:] = mm_rows(inbox, db)
    put_blocks((grads_no, grads_ni), me_ref[0], count, keep_ref, away_ref)


def backward_kernel(
    recv_ref, zeta_ref, slope_ref, normed_ref, inv_ref, dagg_ref, w_edge_out_ref, dye_ref, da_ref
):
    @pl.loop(0, zeta_ref.shape[0] // BLOCK)
    def _(block):
        rows = pl.ds(pl.multiple_of(block * BLOCK, BLOCK), BLOCK)
        up = mm(one_hot_cols(recv_ref[:, rows], dagg_ref.shape[0]), dagg_ref[...])
        dye = norm_back(up, normed_ref[rows].astype(F32), inv_ref[rows]).astype(BF16)
        dye_ref[rows] = dye
        da_ref[rows] = (mm_cols(dye, w_edge_out_ref[...]) * slope_ref[rows].astype(F32)).astype(BF16)


def weights_kernel(
    count,
    slot,
    me_ref,
    send_ref,
    recv_ref,
    halo_ref,
    nodes_ref,
    edges_ref,
    zeta_ref,
    dye_ref,
    da_ref,
    keep_ref,
    away_ref,
    own_ref,
    recv_sums_ref,
    far_ref,
    sums,
    grads_eo,
    grads_ei,
):
    owned, width = nodes_ref.shape
    n_table = sums.shape[0]
    n_far = count * slot
    me = me_ref[0]
    sums[...] = jnp.zeros_like(sums)

    def block_of(device):
        return cube_place(device ^ me, device & 1, count) * slot

    @pl.loop(0, edges_ref.shape[0] // BLOCK)
    def _(block):
        rows = pl.ds(pl.multiple_of(block * BLOCK, BLOCK), BLOCK)
        sender, safe, receiver = edge_ids(rows, owned, slot, send_ref, recv_ref, block_of)
        sums[...] += mm(hot_rows(sender, safe, n_table), da_ref[rows])

    own = sums[:owned].astype(BF16)
    recv = sums[owned : 2 * owned].astype(BF16)
    far = sums[2 * owned : 2 * owned + n_far].astype(BF16)
    own_ref[...] = own
    recv_sums_ref[...] = recv
    far_ref[...] = far
    away_ref[keep_ref.shape[0] :] = far[n_far // 2 :]
    shape = (n_far, count * HALO_ROWS)
    column = lax.broadcasted_iota(jnp.int32, shape, 1)
    device = column // HALO_ROWS
    there = (column % HALO_ROWS < slot) & (
        block_of(device) + column % HALO_ROWS == lax.broadcasted_iota(jnp.int32, shape, 0)
    )
    halo = mm(jnp.where(there, 1.0, 0.0).astype(BF16), halo_ref[...]).astype(BF16)
    nodes = nodes_ref[...]
    for start in range(0, width, TILE):
        cols = slice(start, start + TILE)
        grads_eo[cols] = mm_rows(zeta_ref[:, cols], dye_ref[...])
        grads_ei[cols] = mm_rows(edges_ref[:, cols], da_ref[...])
    grads_ei[width : 2 * width] = mm_rows(nodes, own) + mm_rows(halo, far)
    grads_ei[2 * width :] = mm_rows(nodes, recv)
    put_blocks((grads_eo, grads_ei), me, count, keep_ref, away_ref)


def ride_kernel(step, count, slot, keep_ref, arrived_ref, far_ref, next_keep_ref, next_away_ref, next_far_ref):
    size, half = keep_ref.shape[0], next_keep_ref.shape[0]
    next_keep_ref[...] = keep_ref[:half] + arrived_ref[:half]
    next_away_ref[:half] = keep_ref[half:] + arrived_ref[half:size]
    far = swap_rows(step, count, slot, far_ref[...], arrived_ref[size:])
    next_far_ref[...] = far
    next_away_ref[half:] = mm(take_rows(step + 1, count, slot), far).astype(BF16)


def swap_rows(step, count, slot, far, arrived):
    take = take_rows(step, count, slot)
    stays = 1.0 - jnp.sum(take.astype(F32), axis=0, keepdims=True)
    rows = far.shape[0]
    square = lax.broadcasted_iota(jnp.int32, (rows, rows), 0) == lax.broadcasted_iota(jnp.int32, (rows, rows), 1)
    stay = jnp.where(square, stays, 0.0).astype(BF16)
    return (mm(stay, far) + mm_rows(take, arrived)).astype(BF16)


def node_kernel(own_ref, recv_ref, part_ref, w_send_ref, w_recv_ref, out_ref):
    out_ref[...] = part_ref[...] + mm_cols(own_ref[...], w_send_ref[...]) + mm_cols(recv_ref[...], w_recv_ref[...])


def last_kernel(
    step, count, slot, keep_ref, arrived_ref, far_ref, pick_ref, node_ref, w_send_ref, first_ref, rest_ref, grad_ref
):
    share, rest = first_ref.shape[0], rest_ref.shape[0]
    size = keep_ref.shape[0]
    far = swap_rows(step, count, slot, far_ref[...], arrived_ref[size:])
    total = keep_ref[...].astype(F32) + arrived_ref[:size].astype(F32)
    first_ref[...] = total[:share]
    rest_ref[...] = total[share : share + rest]
    sums = mm_rows(pick_ref[...], far).astype(BF16)
    grad_ref[...] = (node_ref[...] + mm_cols(sums, w_send_ref[...])).astype(BF16)


def add_kernel(keep_ref, arrived_ref, next_keep_ref, next_send_ref):
    half = next_keep_ref.shape[0]
    next_send_ref[...] = keep_ref[half:] + arrived_ref[half:]
    next_keep_ref[...] = keep_ref[:half] + arrived_ref[:half]


def total_kernel(kept_ref, came_ref, first_ref, rest_ref):
    share = first_ref.shape[0]
    total = kept_ref[...].astype(F32) + came_ref[...].astype(F32)
    first_ref[...] = total[:share]
    rest_ref[...] = total[share : share + rest_ref.shape[0]]


VMEM = pl.BlockSpec(memory_space=pltpu.VMEM)
SMEM = pl.BlockSpec(memory_space=pltpu.SMEM)
HBM = pl.BlockSpec(memory_space=pltpu.HBM)
COST = pl.CostEstimate(flops=1 << 10, bytes_accessed=1 << 10, transcendentals=0)


def kernel_call(kernel, name, outs, scratch, args, near=(), far=(), limit=16):
    specs = [SMEM if arg.shape == (1,) else VMEM for arg in args] + [VMEM] * len(near) + [HBM] * len(far)
    near = [pltpu.with_memory_space_constraint(array, pltpu.VMEM) for array in near]
    far = [pltpu.with_memory_space_constraint(array, pltpu.HBM) for array in far]
    return pl.pallas_call(
        kernel,
        out_shape=tuple(outs),
        in_specs=specs,
        out_specs=(VMEM,) * len(outs),
        scratch_shapes=scratch,
        compiler_params=pltpu.CompilerParams(vmem_limit_bytes=limit << 20),
        cost_estimate=COST,
        name=name,
    )(*args, *near, *far)


def in_order(first, then):
    return lax.optimization_barrier((first, then))


def trade(rows):
    return lax.all_to_all(rows, "patch", split_axis=0, concat_axis=0, tiled=True)


def body(
    count,
    nodes,
    edges,
    cot_nodes,
    w_edge_in,
    w_edge_out,
    w_node_in,
    w_node_out,
    send_rows,
    edge_sender,
    edge_receiver,
):
    owned, width = nodes.shape
    n_edges = edges.shape[0]
    slot = send_rows.shape[2]
    share = width // count
    n_halo = count * HALO_ROWS
    me = lax.axis_index("patch").astype(jnp.int32).reshape(1)
    sender = edge_sender.reshape(1, -1)
    receiver = edge_receiver.reshape(1, -1)

    def space(*shape, dtype=BF16):
        return pltpu.VMEM(shape, dtype)

    def block_pair(rows, riders=0):
        size = count // 2 * (-(-(rows * share) // 16) * 16)
        return [space(size, width), space(size + riders, width)]

    n_far = count * slot
    pick, halo_out = kernel_call(
        functools.partial(pick_kernel, count),
        "pick",
        [jax.ShapeDtypeStruct((n_far, owned), BF16), jax.ShapeDtypeStruct((n_halo, width), BF16)],
        [],
        (me, send_rows[0].T, nodes),
        limit=60,
    )
    halo = trade(halo_out)
    base = pl.pallas_call(
        local_kernel,
        out_shape=jax.ShapeDtypeStruct((n_edges, width), F32),
        grid=(n_edges // GRID_BLOCK,),
        in_specs=[
            pl.BlockSpec((1, GRID_BLOCK), lambda i: (0, i)),
            pl.BlockSpec((1, GRID_BLOCK), lambda i: (0, i)),
            pl.BlockSpec((owned, width), lambda i: (0, 0)),
            pl.BlockSpec((3 * width, width), lambda i: (0, 0)),
            pl.BlockSpec((GRID_BLOCK, width), lambda i: (i, 0)),
        ],
        out_specs=pl.BlockSpec((GRID_BLOCK, width), lambda i: (i, 0)),
        scratch_shapes=[space(2 * owned, width)],
        compiler_params=pltpu.CompilerParams(vmem_limit_bytes=60 << 20),
        cost_estimate=COST,
        name="local",
    )(sender, receiver, nodes, w_edge_in, edges)
    rows, square = space(n_edges, width), space(width, width)
    keep1, away1, zeta, slope, normed, inv, dagg, node_part, near_nodes, near_out, near_edges, w_send, w_recv = kernel_call(
        functools.partial(forward_kernel, count, slot),
        "forward",
        block_pair(3)
        + [rows, rows, rows, space(n_edges, 1, dtype=F32)]
        + [space(owned, width), space(owned, width, dtype=F32), space(owned, width), square, rows, square, square],
        [space(n_edges, width, dtype=F32), space(2 * width, width), square, space(owned, width)]
        + [space(n_halo, width)]
        + [space(r, width, dtype=F32) for r in (owned, width, 2 * width)]
        + [pltpu.SemaphoreType.DMA((n_edges // BLOCK,)), pltpu.SemaphoreType.DMA((8,))],
        (me, sender, receiver, halo),
        far=(w_edge_in, base, w_edge_out, nodes, w_node_in, w_node_out, cot_nodes, edges),
        limit=36,
    )

    def add(keep, arrived):
        half = [space(keep.shape[0] // 2, width)] * 2
        return kernel_call(add_kernel, "add", half, [], (keep, arrived), limit=8)

    def ride(step, keep, arrived, far):
        half = keep.shape[0] // 2
        outs = [space(half, width), space(half + n_far // 2, width), space(n_far, width)]
        kernel = functools.partial(ride_kernel, step, count, slot)
        return kernel_call(kernel, "ride", outs, [], (keep, arrived, far), limit=8)

    came1 = cube_permute(away1, 0, count)
    dye, da = kernel_call(
        backward_kernel, "backward", [rows, rows], [], (receiver,), (zeta, slope, normed, inv, dagg, near_out)
    )
    came1, dye = in_order(came1, dye)
    keep1, away1 = add(keep1, came1)
    away1, da = in_order(away1, da)
    came1 = cube_permute(away1, 1, count)
    keep2, away2, own_sums, recv_sums, far_sums = kernel_call(
        functools.partial(weights_kernel, count, slot),
        "weights",
        block_pair(4, n_far // 2) + [space(owned, width), space(owned, width), space(n_far, width)],
        [space(r, width, dtype=F32) for r in (2 * owned + -(-n_far // LANES) * LANES, width, 3 * width)],
        (me, sender, receiver, halo),
        (near_nodes, near_edges, zeta, dye, da),
    )
    keep1, away1 = add(keep1, came1)
    away1, away2 = in_order(away1, away2)
    came1 = cube_permute(away1, 2, count)
    came2 = cube_permute(away2, 0, count)
    keep2, away2, far_sums = ride(0, keep2, came2, far_sums)
    came2 = cube_permute(away2, 1, count)
    steps = count.bit_length() - 1
    for step in range(3, steps):
        keep1, away1 = add(keep1, came1)
        came1 = cube_permute(away1, step, count)
    _, da = in_order(away1, da)
    edge_grad = mm_cols(da, w_edge_in[:width]).astype(BF16)
    edge_grad, came2 = in_order(edge_grad, came2)
    for step in range(2, steps):
        keep2, away2, far_sums = ride(step - 1, keep2, came2, far_sums)
        came2 = cube_permute(away2, step, count)
    away2, own_sums = in_order(away2, own_sums)
    node_sum = kernel_call(
        node_kernel, "node", [space(owned, width, dtype=F32)], [], (own_sums, recv_sums, node_part, w_send, w_recv)
    )[0]

    def whole(*parts):
        return [jax.ShapeDtypeStruct((part * share, width), F32) for part in parts]

    node_out, node_in = kernel_call(total_kernel, "node_total", whole(1, 2), [], (keep1, came1), limit=8)
    node_out, came2 = in_order(node_out, came2)
    edge_out, edge_in, node_grad = kernel_call(
        functools.partial(last_kernel, steps - 1, count, slot),
        "last",
        whole(1, 3) + [jax.ShapeDtypeStruct((owned, width), BF16)],
        [],
        (keep2, came2, far_sums, pick, node_sum, w_send),
        limit=8,
    )
    return node_grad, edge_grad, edge_in, edge_out, node_in, node_out


def solution(mesh):
    rows = P(("groups", "patch"), None)
    flat = P(("groups", "patch"))
    return jax.shard_map(
        functools.partial(body, mesh.shape["patch"]),
        mesh=mesh,
        in_specs=(rows, rows, rows, P(), P(), P(), P(), P(("groups", "patch"), None, None), flat, flat),
        out_specs=(rows,) * 6,
        check_vma=False,
    )
```

```python
import functools

import jax
import jax.numpy as jnp
from jax import lax
from jax.experimental import pallas as pl
from jax.experimental.pallas import tpu as pltpu
from jax.sharding import PartitionSpec as P

BF16 = jnp.bfloat16
F32 = jnp.float32
EPS = 1e-05
LANES = 128
BLOCK = 1024
TILE = 256
HALO_ROWS = 8


def mm(left, right):
    return jnp.dot(left, right, preferred_element_type=F32)


def mm_rows(left, right):
    return lax.dot_general(left, right, (((0,), (0,)), ((), ())), preferred_element_type=F32)


def mm_cols(left, right):
    return lax.dot_general(left, right, (((1,), (1,)), ((), ())), preferred_element_type=F32)


def sigmoid(values):
    return 0.5 * jnp.tanh(0.5 * values) + 0.5


def normalize(values):
    center = values - jnp.mean(values, axis=-1, keepdims=True)
    inv_std = lax.rsqrt(jnp.mean(center * center, axis=-1, keepdims=True) + EPS)
    return center * inv_std, inv_std


def norm_back(upstream, normed, inv_std):
    return inv_std * (
        upstream
        - jnp.mean(upstream, axis=-1, keepdims=True)
        - normed * jnp.mean(upstream * normed, axis=-1, keepdims=True)
    )


def cube_masks(count):
    return [1 << i for i in range(count.bit_length() - 1)]


def cube_orders(count):
    rest = list(range(1, count.bit_length() - 1))
    return [0] + rest, [0] + rest[:2][::-1] + rest[2:]


def cube_place(apart, parity, count):
    bits = count.bit_length() - 1
    coords = [(apart >> i) & 1 for i in range(bits)]
    even, odd = [sum(coords[dim] << (bits - 1 - j) for j, dim in enumerate(order)) for order in cube_orders(count)]
    return jnp.where(parity == 0, even, odd)


def cube_permute(blocks, step, count):
    mask, orders = cube_masks(count), cube_orders(count)
    pairs = [(i, i ^ mask[orders[i & 1][step]]) for i in range(count)]
    return lax.ppermute(blocks, "patch", pairs)


def one_hot_cols(ids, width):
    rows = ids.shape[1]
    spread = jnp.transpose(jnp.broadcast_to(ids, (LANES, rows)))
    lane = lax.broadcasted_iota(jnp.int32, (rows, LANES), 1)
    tiles = [jnp.where(spread == lane + start, 1.0, 0.0).astype(BF16) for start in range(0, width, LANES)]
    return jnp.concatenate(tiles, axis=1)[:, :width]


def hot_cols(first, second, width):
    rows = first.shape[1]
    left = jnp.transpose(jnp.broadcast_to(first, (LANES, rows)))
    right = jnp.transpose(jnp.broadcast_to(second, (LANES, rows)))
    lane = lax.broadcasted_iota(jnp.int32, (rows, LANES), 1)
    tiles = [
        jnp.where((left == lane + start) | (right == lane + start), 1.0, 0.0).astype(BF16)
        for start in range(0, width, LANES)
    ]
    return jnp.concatenate(tiles, axis=1)


def hot_rows(first, second, width):
    row = lax.broadcasted_iota(jnp.int32, (width, first.shape[1]), 0)
    return jnp.where((row == first) | (row == second), 1.0, 0.0).astype(BF16)


def edge_ids(rows, owned, slot, send_ref, recv_ref, block_of):
    sender = send_ref[:, rows]
    receiver = recv_ref[:, rows]
    far = sender - owned
    sender = jnp.where(far < 0, sender, 2 * owned + block_of(far // slot) + far % slot)
    return sender, jnp.maximum(receiver, 0) + owned, receiver


def take_rows(step, count, slot):
    weight = count >> (step + 1)
    shape = (count // 2 * slot, count * slot)
    out = lax.broadcasted_iota(jnp.int32, shape, 0)
    block, row = out // slot, out % slot
    place = block // weight * 2 * weight + weight + block % weight
    return jnp.where(lax.broadcasted_iota(jnp.int32, shape, 1) == place * slot + row, 1.0, 0.0).astype(BF16)


def put_blocks(sources, me, count, keep_ref, send_ref):
    shares = [source.shape[0] // count for source in sources]
    half = count // 2
    size = keep_ref.shape[0] // half
    spare = size - sum(shares)
    bits = count.bit_length() - 1
    for place in range(count):
        apart = [
            sum(((place >> (bits - 1 - j)) & 1) << dim for j, dim in enumerate(order)) for order in cube_orders(count)
        ]
        odd_target = (me ^ (place // half)) & 1
        target = me ^ jnp.where(odd_target == 0, *apart)
        parts = [
            source[pl.ds(pl.multiple_of(target * share, share), share)] for source, share in zip(sources, shares)
        ]
        if spare:
            parts.append(jnp.zeros((spare, keep_ref.shape[1]), F32))
        start = place % half * size
        (keep_ref if place < half else send_ref)[start : start + size] = jnp.concatenate(parts, axis=0).astype(BF16)


def pick_kernel(count, picks_ref, nodes_ref, pick_ref, rows_ref):
    slot = picks_ref.shape[0]
    owned = nodes_ref.shape[0]
    me = lax.axis_index("patch")

    def choose(rows, start):
        shape = (rows, count)
        row = lax.broadcasted_iota(jnp.int32, shape, 0)
        first = start(lax.broadcasted_iota(jnp.int32, shape, 1))
        ids = jnp.zeros(shape, jnp.int32)
        for place in range(slot):
            ids = ids + jnp.where(row == first + place, picks_ref[place : place + 1] + 1, 0)
        ids = jnp.sum(ids.astype(F32), axis=1, keepdims=True).astype(jnp.int32) - 1
        node = lax.broadcasted_iota(jnp.int32, (rows, owned), 1)
        return jnp.where(node == ids, 1.0, 0.0).astype(BF16)

    rows_ref[...] = mm(choose(count * HALO_ROWS, lambda device: device * HALO_ROWS), nodes_ref[...]).astype(BF16)
    pick_ref[...] = choose(count * slot, lambda device: cube_place(device ^ me, me & 1, count) * slot)


def local_kernel(
    nodes_far, w_edge_in_far, w_edge_out_far, nodes_ref, w_send, w_self, w_edge_out_ref, table, w_recv, sems
):
    owned, width = nodes_ref.shape
    pairs = (
        (nodes_far, nodes_ref),
        (w_edge_in_far.at[width : 2 * width], w_send),
        (w_edge_in_far.at[2 * width :], w_recv),
        (w_edge_in_far.at[:width], w_self),
        (w_edge_out_far, w_edge_out_ref),
    )
    copies = [pltpu.make_async_copy(src, dst, sems.at[i]) for i, (src, dst) in enumerate(pairs)]
    for copy in copies:
        copy.start()
    copies[0].wait()
    nodes = nodes_ref[...]
    copies[1].wait()
    table[:owned] = mm(nodes, w_send[...]).astype(BF16)
    copies[2].wait()
    table[owned:] = mm(nodes, w_recv[...]).astype(BF16)
    for copy in copies[3:]:
        copy.wait()


def forward_kernel(
    count,
    slot,
    halo_ref,
    nodes_ref,
    w_send,
    w_self,
    w_edge_out_ref,
    own_table,
    edges_far,
    send_far,
    recv_far,
    w_node_in_far,
    w_node_out_far,
    cot_far,
    w_edge_in_far,
    keep_ref,
    away_ref,
    zeta_ref,
    slope_ref,
    normed_ref,
    inv_ref,
    dagg_ref,
    node_part_ref,
    edges_ref,
    w_recv,
    send_ref,
    recv_ref,
    w_node_in_ref,
    w_node_out_ref,
    cot_ref,
    table,
    agg,
    grads_no,
    grads_ni,
    edge_sems,
    sems,
):
    owned, width = nodes_ref.shape
    n_table = table.shape[0]
    n_blocks = edges_ref.shape[0] // BLOCK

    def block_rows(block):
        return pl.ds(pl.multiple_of(block * BLOCK, BLOCK), BLOCK)

    def edge_copy(block):
        rows = block_rows(block)
        return pltpu.make_async_copy(edges_far.at[rows], edges_ref.at[rows], edge_sems.at[block])

    pairs = (
        (send_far, send_ref),
        (recv_far, recv_ref),
        (w_node_in_far, w_node_in_ref),
        (w_node_out_far, w_node_out_ref),
        (cot_far, cot_ref),
        (w_edge_in_far.at[2 * width :], w_recv),
    )
    copies = [pltpu.make_async_copy(src, dst, sems.at[i]) for i, (src, dst) in enumerate(pairs)]
    for copy in copies[:2]:
        copy.start()

    @pl.loop(0, n_blocks)
    def _(block):
        edge_copy(block).start()

    for copy in copies[2:]:
        copy.start()
    agg[...] = jnp.zeros_like(agg)
    nodes = nodes_ref[...]
    table[: 2 * owned] = own_table[...]
    table[2 * owned :] = mm(halo_ref[...], w_send[...]).astype(BF16)
    for copy in copies[:2]:
        copy.wait()

    @pl.loop(0, n_blocks)
    def _(block):
        rows = block_rows(block)
        edge_copy(block).wait()
        sender, safe, receiver = edge_ids(rows, owned, slot, send_ref, recv_ref, lambda device: device * HALO_ROWS)
        pre = mm(edges_ref[rows], w_self[...]) + mm(hot_cols(sender, safe, n_table), table[...])
        sigma = sigmoid(pre)
        zed = (pre * sigma).astype(BF16)
        zeta_ref[rows] = zed
        slope_ref[rows] = (sigma * (1.0 + pre * (1.0 - sigma))).astype(BF16)
        unit, inv_std = normalize(mm(zed, w_edge_out_ref[...]))
        message = unit.astype(BF16)
        normed_ref[rows] = message
        inv_ref[rows] = inv_std
        agg[...] += mm(hot_rows(receiver, receiver, owned), message)

    for copy in copies[2:]:
        copy.wait()
    inbox = agg[...].astype(BF16)
    pre = mm(nodes, w_node_in_ref[:width]) + mm(inbox, w_node_in_ref[width:])
    sigma = sigmoid(pre)
    zed = (pre * sigma).astype(BF16)
    unit, inv_std = normalize(mm(zed, w_node_out_ref[...]))
    upstream = cot_ref[...].astype(F32)
    dy = norm_back(upstream, unit, inv_std).astype(BF16)
    db = (mm_cols(dy, w_node_out_ref[...]) * (sigma * (1.0 + pre * (1.0 - sigma)))).astype(BF16)
    dagg_ref[...] = mm_cols(db, w_node_in_ref[width:]).astype(BF16)
    node_part_ref[...] = upstream + mm_cols(db, w_node_in_ref[:width])
    grads_no[...] = mm_rows(zed, dy)
    grads_ni[:width] = mm_rows(nodes, db)
    grads_ni[width:] = mm_rows(inbox, db)
    put_blocks((grads_no, grads_ni), lax.axis_index("patch"), count, keep_ref, away_ref)


def backward_kernel(
    recv_ref, zeta_ref, slope_ref, normed_ref, inv_ref, dagg_ref, w_edge_out_ref, dye_ref, da_ref
):
    @pl.loop(0, zeta_ref.shape[0] // BLOCK)
    def _(block):
        rows = pl.ds(pl.multiple_of(block * BLOCK, BLOCK), BLOCK)
        up = mm(one_hot_cols(recv_ref[:, rows], dagg_ref.shape[0]), dagg_ref[...])
        dye = norm_back(up, normed_ref[rows].astype(F32), inv_ref[rows]).astype(BF16)
        dye_ref[rows] = dye
        da_ref[rows] = (mm_cols(dye, w_edge_out_ref[...]) * slope_ref[rows].astype(F32)).astype(BF16)


def weights_kernel(
    count,
    slot,
    halo_ref,
    send_ref,
    recv_ref,
    nodes_ref,
    edges_ref,
    zeta_ref,
    dye_ref,
    da_ref,
    keep_ref,
    away_ref,
    own_ref,
    recv_sums_ref,
    far_ref,
    sums,
    grads_eo,
    grads_ei,
):
    owned, width = nodes_ref.shape
    n_table = sums.shape[0]
    n_far = count * slot
    me = lax.axis_index("patch")

    def block_of(device):
        return cube_place(device ^ me, device & 1, count) * slot

    sender, safe, _ = edge_ids(slice(None), owned, slot, send_ref, recv_ref, block_of)
    sums[...] = mm(hot_rows(sender, safe, n_table), da_ref[...])

    own = sums[:owned].astype(BF16)
    recv = sums[owned : 2 * owned].astype(BF16)
    far = sums[2 * owned : 2 * owned + n_far].astype(BF16)
    own_ref[...] = own
    recv_sums_ref[...] = recv
    far_ref[...] = far
    away_ref[keep_ref.shape[0] :] = far[n_far // 2 :]
    shape = (n_far, count * HALO_ROWS)
    column = lax.broadcasted_iota(jnp.int32, shape, 1)
    device = column // HALO_ROWS
    there = (column % HALO_ROWS < slot) & (
        block_of(device) + column % HALO_ROWS == lax.broadcasted_iota(jnp.int32, shape, 0)
    )
    halo = mm(jnp.where(there, 1.0, 0.0).astype(BF16), halo_ref[...]).astype(BF16)
    nodes = nodes_ref[...]
    for start in range(0, width, TILE):
        cols = slice(start, start + TILE)
        grads_eo[cols] = mm_rows(zeta_ref[:, cols], dye_ref[...])
        grads_ei[cols] = mm_rows(edges_ref[:, cols], da_ref[...])
    grads_ei[width : 2 * width] = mm_rows(nodes, own) + mm_rows(halo, far)
    grads_ei[2 * width :] = mm_rows(nodes, recv)
    put_blocks((grads_eo, grads_ei), me, count, keep_ref, away_ref)


def ride_kernel(step, count, slot, keep_ref, arrived_ref, far_ref, next_keep_ref, next_away_ref, next_far_ref):
    size, half = keep_ref.shape[0], next_keep_ref.shape[0]
    next_keep_ref[...] = keep_ref[:half] + arrived_ref[:half]
    next_away_ref[:half] = keep_ref[half:] + arrived_ref[half:size]
    far = swap_rows(step, count, slot, far_ref[...], arrived_ref[size:])
    next_far_ref[...] = far
    next_away_ref[half:] = mm(take_rows(step + 1, count, slot), far).astype(BF16)


def swap_rows(step, count, slot, far, arrived):
    take = take_rows(step, count, slot)
    stays = 1.0 - jnp.sum(take.astype(F32), axis=0, keepdims=True)
    rows = far.shape[0]
    square = lax.broadcasted_iota(jnp.int32, (rows, rows), 0) == lax.broadcasted_iota(jnp.int32, (rows, rows), 1)
    stay = jnp.where(square, stays, 0.0).astype(BF16)
    return (mm(stay, far) + mm_rows(take, arrived)).astype(BF16)


def node_kernel(own_ref, recv_ref, part_ref, w_send_ref, w_recv_ref, out_ref):
    out_ref[...] = part_ref[...] + mm_cols(own_ref[...], w_send_ref[...]) + mm_cols(recv_ref[...], w_recv_ref[...])


def last_kernel(
    step, count, slot, keep_ref, arrived_ref, far_ref, pick_ref, node_ref, w_send_ref, first_ref, rest_ref, grad_ref
):
    share, rest = first_ref.shape[0], rest_ref.shape[0]
    size = keep_ref.shape[0]
    far = swap_rows(step, count, slot, far_ref[...], arrived_ref[size:])
    total = keep_ref[...].astype(F32) + arrived_ref[:size].astype(F32)
    first_ref[...] = total[:share]
    rest_ref[...] = total[share : share + rest]
    far = mm_cols(far, w_send_ref[...]).astype(BF16)
    grad_ref[...] = (node_ref[...] + mm_rows(pick_ref[...], far)).astype(BF16)


def add_kernel(keep_ref, arrived_ref, next_keep_ref, next_send_ref):
    half = next_keep_ref.shape[0]
    next_send_ref[...] = keep_ref[half:] + arrived_ref[half:]
    next_keep_ref[...] = keep_ref[:half] + arrived_ref[:half]


def total_kernel(kept_ref, came_ref, first_ref, rest_ref):
    share = first_ref.shape[0]
    total = kept_ref[...].astype(F32) + came_ref[...].astype(F32)
    first_ref[...] = total[:share]
    rest_ref[...] = total[share : share + rest_ref.shape[0]]


VMEM = pl.BlockSpec(memory_space=pltpu.VMEM)
HBM = pl.BlockSpec(memory_space=pltpu.HBM)
COST = pl.CostEstimate(flops=1 << 10, bytes_accessed=1 << 10, transcendentals=0)
LARGE_COST = pl.CostEstimate(flops=1 << 10, bytes_accessed=1 << 26, transcendentals=0)


def kernel_call(kernel, name, outs, scratch, args, near=(), far=(), limit=16, cost=COST, out_spec=None):
    specs = [VMEM] * (len(args) + len(near)) + [HBM] * len(far)
    near = [pltpu.with_memory_space_constraint(array, pltpu.VMEM) for array in near]
    far = [pltpu.with_memory_space_constraint(array, pltpu.HBM) for array in far]
    return pl.pallas_call(
        kernel,
        out_shape=tuple(outs),
        in_specs=specs,
        out_specs=(out_spec or VMEM,) * len(outs),
        scratch_shapes=scratch,
        compiler_params=pltpu.CompilerParams(vmem_limit_bytes=limit << 20),
        cost_estimate=cost,
        name=name,
    )(*args, *near, *far)


def in_order(first, then):
    return lax.optimization_barrier((first, then))


def trade(rows):
    return lax.all_to_all(rows, "patch", split_axis=0, concat_axis=0, tiled=True)


def body(
    count,
    nodes,
    edges,
    cot_nodes,
    w_edge_in,
    w_edge_out,
    w_node_in,
    w_node_out,
    send_rows,
    edge_sender,
    edge_receiver,
):
    owned, width = nodes.shape
    n_edges = edges.shape[0]
    slot = send_rows.shape[2]
    share = width // count
    n_halo = count * HALO_ROWS
    sender = edge_sender.reshape(1, -1)
    receiver = edge_receiver.reshape(1, -1)

    def space(*shape, dtype=BF16):
        return pltpu.VMEM(shape, dtype)

    def block_pair(rows, riders=0):
        size = count // 2 * (-(-(rows * share) // 16) * 16)
        return [space(size, width), space(size + riders, width)]

    n_far = count * slot
    pick, halo_out = kernel_call(
        functools.partial(pick_kernel, count),
        "pick",
        [jax.ShapeDtypeStruct((n_far, owned), BF16), jax.ShapeDtypeStruct((n_halo, width), BF16)],
        [],
        (send_rows[0].T, nodes),
        limit=60,
    )
    halo = trade(halo_out)
    rows, square, ids = space(n_edges, width), space(width, width), space(1, n_edges, dtype=jnp.int32)
    near = kernel_call(
        local_kernel,
        "local",
        [space(owned, width), square, square, square, space(2 * owned, width)],
        [square, pltpu.SemaphoreType.DMA((5,))],
        (),
        far=(nodes, w_edge_in, w_edge_out),
    )
    near_nodes, w_send, _, near_out, _ = near
    keep1, away1, zeta, slope, normed, inv, dagg, node_part, near_edges, w_recv, sender, receiver = kernel_call(
        functools.partial(forward_kernel, count, slot),
        "forward",
        block_pair(3)
        + [rows, rows, rows, space(n_edges, 1, dtype=F32)]
        + [space(owned, width), space(owned, width, dtype=F32), rows, square, ids, ids],
        [space(2 * width, width), square, space(owned, width), space(2 * owned + n_halo, width)]
        + [space(r, width, dtype=F32) for r in (owned, width, 2 * width)]
        + [pltpu.SemaphoreType.DMA((n_edges // BLOCK,)), pltpu.SemaphoreType.DMA((6,))],
        (halo,),
        near=near,
        far=(edges, sender, receiver, w_node_in, w_node_out, cot_nodes, w_edge_in),
        limit=36,
    )

    def add(keep, arrived):
        half = [space(keep.shape[0] // 2, width)] * 2
        return kernel_call(add_kernel, "add", half, [], (keep, arrived), limit=8, cost=LARGE_COST)

    def ride(step, keep, arrived, far):
        half = keep.shape[0] // 2
        outs = [space(half, width), space(half + n_far // 2, width), space(n_far, width)]
        kernel = functools.partial(ride_kernel, step, count, slot)
        return kernel_call(kernel, "ride", outs, [], (keep, arrived, far), limit=8)

    came1 = cube_permute(away1, 0, count)
    dye, da = kernel_call(
        backward_kernel, "backward", [rows, rows], [], (), (receiver, zeta, slope, normed, inv, dagg, near_out)
    )
    came1, dye = in_order(came1, dye)
    keep1, away1 = add(keep1, came1)
    away1, da = in_order(away1, da)
    came1 = cube_permute(away1, 1, count)
    keep2, away2, own_sums, recv_sums, far_sums = kernel_call(
        functools.partial(weights_kernel, count, slot),
        "weights",
        block_pair(4, n_far // 2) + [space(owned, width), space(owned, width), space(n_far, width)],
        [space(r, width, dtype=F32) for r in (2 * owned + -(-n_far // LANES) * LANES, width, 3 * width)],
        (halo,),
        (sender, receiver, near_nodes, near_edges, zeta, dye, da),
    )
    steps = count.bit_length() - 1
    for step in range(1, steps - 1):
        keep1, away1 = add(keep1, came1)
        if step == 1:
            away1, away2 = in_order(away1, away2)
            came2 = cube_permute(away2, 0, count)
        else:
            away1, came2 = in_order(away1, came2)
        came1 = cube_permute(away1, step + 1, count)
        keep2, away2, far_sums = ride(step - 1, keep2, came2, far_sums)
        came2 = cube_permute(away2, step, count)
    keep2, away2, far_sums = ride(steps - 2, keep2, came2, far_sums)
    came1, away2 = in_order(came1, away2)
    _, (da, own_sums) = in_order(away2, (da, own_sums))
    came2 = cube_permute(away2, steps - 1, count)
    edge_grad = mm_cols(da, w_edge_in[:width]).astype(BF16)
    node_sum = kernel_call(
        node_kernel, "node", [space(owned, width, dtype=F32)], [], (own_sums, recv_sums, node_part, w_send, w_recv)
    )[0]

    def whole(*parts):
        return [jax.ShapeDtypeStruct((part * share, width), F32) for part in parts]

    node_out, node_in = kernel_call(total_kernel, "node_total", whole(1, 2), [], (keep1, came1), limit=8)
    edge_out, edge_in, node_grad = kernel_call(
        functools.partial(last_kernel, steps - 1, count, slot),
        "last",
        whole(1, 3) + [jax.ShapeDtypeStruct((owned, width), BF16)],
        [],
        (keep2, came2, far_sums, pick, node_sum, w_send),
        limit=8,
    )
    return node_grad, edge_grad, edge_in, edge_out, node_in, node_out


def solution(mesh):
    rows = P(("groups", "patch"), None)
    flat = P(("groups", "patch"))
    return jax.shard_map(
        functools.partial(body, mesh.shape["patch"]),
        mesh=mesh,
        in_specs=(rows, rows, rows, P(), P(), P(), P(), P(("groups", "patch"), None, None), flat, flat),
        out_specs=(rows,) * 6,
        check_vma=False,
    )
```

```python
import functools

import jax
import jax.numpy as jnp
from jax import lax
from jax.experimental import pallas as pl
from jax.experimental.pallas import tpu as pltpu
from jax.sharding import PartitionSpec as P

BF16 = jnp.bfloat16
F32 = jnp.float32
EPS = 1e-05
LANES = 128
TILE = 256
HALO_ROWS = 8


def mm(left, right):
    return jnp.dot(left, right, preferred_element_type=F32)


def mm_rows(left, right):
    return lax.dot_general(left, right, (((0,), (0,)), ((), ())), preferred_element_type=F32)


def mm_cols(left, right):
    return lax.dot_general(left, right, (((1,), (1,)), ((), ())), preferred_element_type=F32)


def sigmoid(values):
    return 0.5 * jnp.tanh(0.5 * values) + 0.5


def normalize(values):
    center = values - jnp.mean(values, axis=-1, keepdims=True)
    inv_std = lax.rsqrt(jnp.mean(center * center, axis=-1, keepdims=True) + EPS)
    return center * inv_std, inv_std


def norm_back(upstream, normed, inv_std):
    return inv_std * (
        upstream
        - jnp.mean(upstream, axis=-1, keepdims=True)
        - normed * jnp.mean(upstream * normed, axis=-1, keepdims=True)
    )


def cube_masks(count):
    return [1 << i for i in range(count.bit_length() - 1)]


def cube_orders(count):
    rest = list(range(1, count.bit_length() - 1))
    return [0] + rest, [0] + rest[:2][::-1] + rest[2:]


def cube_place(apart, parity, count):
    bits = count.bit_length() - 1
    coords = [(apart >> i) & 1 for i in range(bits)]
    even, odd = [sum(coords[dim] << (bits - 1 - j) for j, dim in enumerate(order)) for order in cube_orders(count)]
    return jnp.where(parity == 0, even, odd)


def cube_permute(blocks, step, count):
    mask, orders = cube_masks(count), cube_orders(count)
    pairs = [(i, i ^ mask[orders[i & 1][step]]) for i in range(count)]
    return lax.ppermute(blocks, "patch", pairs)


def one_hot_cols(ids, width):
    rows = ids.shape[1]
    spread = jnp.transpose(jnp.broadcast_to(ids, (LANES, rows)))
    lane = lax.broadcasted_iota(jnp.int32, (rows, LANES), 1)
    tiles = [jnp.where(spread == lane + start, 1.0, 0.0).astype(BF16) for start in range(0, width, LANES)]
    return jnp.concatenate(tiles, axis=1)[:, :width]


def hot_cols(first, second, width):
    rows = first.shape[1]
    left = jnp.transpose(jnp.broadcast_to(first, (LANES, rows)))
    right = jnp.transpose(jnp.broadcast_to(second, (LANES, rows)))
    lane = lax.broadcasted_iota(jnp.int32, (rows, LANES), 1)
    tiles = [
        jnp.where((left == lane + start) | (right == lane + start), 1.0, 0.0).astype(BF16)
        for start in range(0, width, LANES)
    ]
    return jnp.concatenate(tiles, axis=1)


def hot_rows(first, second, width):
    row = lax.broadcasted_iota(jnp.int32, (width, first.shape[1]), 0)
    return jnp.where((row == first) | (row == second), 1.0, 0.0).astype(BF16)


def edge_ids(rows, owned, slot, send_ref, recv_ref, block_of):
    sender = send_ref[:, rows]
    receiver = recv_ref[:, rows]
    far = sender - owned
    sender = jnp.where(far < 0, sender, 2 * owned + block_of(far // slot) + far % slot)
    return sender, jnp.maximum(receiver, 0) + owned, receiver


def take_rows(step, count, slot):
    weight = count >> (step + 1)
    shape = (count // 2 * slot, count * slot)
    out = lax.broadcasted_iota(jnp.int32, shape, 0)
    block, row = out // slot, out % slot
    place = block // weight * 2 * weight + weight + block % weight
    return jnp.where(lax.broadcasted_iota(jnp.int32, shape, 1) == place * slot + row, 1.0, 0.0).astype(BF16)


def put_blocks(sources, me, count, keep_ref, send_ref):
    shares = [source.shape[0] // count for source in sources]
    half = count // 2
    size = keep_ref.shape[0] // half
    spare = size - sum(shares)
    bits = count.bit_length() - 1
    for place in range(count):
        apart = [
            sum(((place >> (bits - 1 - j)) & 1) << dim for j, dim in enumerate(order)) for order in cube_orders(count)
        ]
        odd_target = (me ^ (place // half)) & 1
        target = me ^ jnp.where(odd_target == 0, *apart)
        parts = [
            source[pl.ds(pl.multiple_of(target * share, share), share)] for source, share in zip(sources, shares)
        ]
        if spare:
            parts.append(jnp.zeros((spare, keep_ref.shape[1]), F32))
        start = place % half * size
        (keep_ref if place < half else send_ref)[start : start + size] = jnp.concatenate(parts, axis=0).astype(BF16)


def pick_kernel(count, picks_ref, nodes_ref, pick_ref, rows_ref):
    slot = picks_ref.shape[0]
    owned = nodes_ref.shape[0]
    me = lax.axis_index("patch")

    def choose(rows, start):
        shape = (rows, count)
        row = lax.broadcasted_iota(jnp.int32, shape, 0)
        first = start(lax.broadcasted_iota(jnp.int32, shape, 1))
        ids = jnp.zeros(shape, jnp.int32)
        for place in range(slot):
            ids = ids + jnp.where(row == first + place, picks_ref[place : place + 1] + 1, 0)
        ids = jnp.sum(ids.astype(F32), axis=1, keepdims=True).astype(jnp.int32) - 1
        node = lax.broadcasted_iota(jnp.int32, (rows, owned), 1)
        return jnp.where(node == ids, 1.0, 0.0).astype(BF16)

    rows_ref[...] = mm(choose(count * HALO_ROWS, lambda device: device * HALO_ROWS), nodes_ref[...]).astype(BF16)
    pick_ref[...] = choose(count * slot, lambda device: cube_place(device ^ me, me & 1, count) * slot)


def local_kernel(
    nodes_far,
    w_edge_in_far,
    w_edge_out_far,
    edges_far,
    nodes_ref,
    w_send,
    w_self,
    w_edge_out_ref,
    table,
    edges1_ref,
    w_recv,
    sems,
):
    owned, width = nodes_ref.shape
    pairs = (
        (nodes_far, nodes_ref),
        (w_edge_in_far.at[width : 2 * width], w_send),
        (w_edge_in_far.at[2 * width :], w_recv),
        (w_edge_in_far.at[:width], w_self),
        (w_edge_out_far, w_edge_out_ref),
        (edges_far.at[: edges1_ref.shape[0]], edges1_ref),
    )
    copies = [pltpu.make_async_copy(src, dst, sems.at[i]) for i, (src, dst) in enumerate(pairs)]
    for copy in copies:
        copy.start()
    copies[0].wait()
    nodes = nodes_ref[...]
    copies[1].wait()
    table[:owned] = mm(nodes, w_send[...]).astype(BF16)
    copies[2].wait()
    table[owned:] = mm(nodes, w_recv[...]).astype(BF16)
    for copy in copies[3:]:
        copy.wait()


def forward_kernel(
    count,
    slot,
    halo_ref,
    nodes_ref,
    w_send,
    w_self,
    w_edge_out_ref,
    own_table,
    edges1_ref,
    edges_far,
    send_far,
    recv_far,
    w_node_in_far,
    w_node_out_far,
    cot_far,
    w_edge_in_far,
    keep_ref,
    away_ref,
    zeta_ref,
    slope_ref,
    normed_ref,
    inv_ref,
    dagg_ref,
    node_part_ref,
    edges2_ref,
    w_recv,
    send_ref,
    recv_ref,
    w_node_in_ref,
    w_node_out_ref,
    cot_ref,
    table,
    agg,
    grads_no,
    grads_ni,
    sems,
):
    owned, width = nodes_ref.shape
    n_table = table.shape[0]
    half = edges1_ref.shape[0]
    pairs = (
        (send_far, send_ref),
        (recv_far, recv_ref),
        (edges_far.at[half:], edges2_ref),
        (w_node_in_far, w_node_in_ref),
        (w_node_out_far, w_node_out_ref),
        (cot_far, cot_ref),
        (w_edge_in_far.at[2 * width :], w_recv),
    )
    copies = [pltpu.make_async_copy(src, dst, sems.at[i]) for i, (src, dst) in enumerate(pairs)]
    for copy in copies:
        copy.start()
    nodes = nodes_ref[...]
    table[: 2 * owned] = own_table[...]
    table[2 * owned :] = mm(halo_ref[...], w_send[...]).astype(BF16)
    for copy in copies[:2]:
        copy.wait()
    for part, edges_ref in enumerate((edges1_ref, edges2_ref)):
        if part:
            copies[2].wait()
        rows = slice(part * half, (part + 1) * half)
        sender, safe, receiver = edge_ids(rows, owned, slot, send_ref, recv_ref, lambda device: device * HALO_ROWS)
        pre = mm(edges_ref[...], w_self[...]) + mm(hot_cols(sender, safe, n_table), table[...])
        sigma = sigmoid(pre)
        zed = (pre * sigma).astype(BF16)
        zeta_ref[rows] = zed
        slope_ref[rows] = (sigma * (1.0 + pre * (1.0 - sigma))).astype(BF16)
        unit, inv_std = normalize(mm(zed, w_edge_out_ref[...]))
        message = unit.astype(BF16)
        normed_ref[rows] = message
        inv_ref[rows] = inv_std
        gathered = mm(hot_rows(receiver, receiver, owned), message)
        agg[...] = agg[...] + gathered if part else gathered

    for copy in copies[3:]:
        copy.wait()
    inbox = agg[...].astype(BF16)
    pre = mm(nodes, w_node_in_ref[:width]) + mm(inbox, w_node_in_ref[width:])
    sigma = sigmoid(pre)
    zed = (pre * sigma).astype(BF16)
    unit, inv_std = normalize(mm(zed, w_node_out_ref[...]))
    upstream = cot_ref[...].astype(F32)
    dy = norm_back(upstream, unit, inv_std).astype(BF16)
    db = (mm_cols(dy, w_node_out_ref[...]) * (sigma * (1.0 + pre * (1.0 - sigma)))).astype(BF16)
    dagg_ref[...] = mm_cols(db, w_node_in_ref[width:]).astype(BF16)
    node_part_ref[...] = upstream + mm_cols(db, w_node_in_ref[:width])
    grads_no[...] = mm_rows(zed, dy)
    grads_ni[:width] = mm_rows(nodes, db)
    grads_ni[width:] = mm_rows(inbox, db)
    put_blocks((grads_no, grads_ni), lax.axis_index("patch"), count, keep_ref, away_ref)


def backward_kernel(
    first, recv_ref, zeta_ref, slope_ref, normed_ref, inv_ref, dagg_ref, w_edge_out_ref, dye_ref, da_ref
):
    rows = slice(first, first + dye_ref.shape[0])
    up = mm(one_hot_cols(recv_ref[:, rows], dagg_ref.shape[0]), dagg_ref[...])
    dye = norm_back(up, normed_ref[rows].astype(F32), inv_ref[rows]).astype(BF16)
    dye_ref[...] = dye
    da_ref[...] = (mm_cols(dye, w_edge_out_ref[...]) * slope_ref[rows].astype(F32)).astype(BF16)


def weights_kernel(
    count,
    slot,
    halo_ref,
    send_ref,
    recv_ref,
    nodes_ref,
    edges1_ref,
    edges2_ref,
    zeta_ref,
    dye1_ref,
    dye2_ref,
    da1_ref,
    da2_ref,
    keep_ref,
    away_ref,
    own_ref,
    recv_sums_ref,
    far_ref,
    sums,
    grads_eo,
    grads_ei,
):
    owned, width = nodes_ref.shape
    n_table = sums.shape[0]
    n_far = count * slot
    me = lax.axis_index("patch")

    def block_of(device):
        return cube_place(device ^ me, device & 1, count) * slot

    half = da1_ref.shape[0]
    sender, safe, _ = edge_ids(slice(None), owned, slot, send_ref, recv_ref, block_of)
    hot = hot_rows(sender, safe, n_table)
    sums[...] = mm(hot[:, :half], da1_ref[...]) + mm(hot[:, half:], da2_ref[...])

    own = sums[:owned].astype(BF16)
    recv = sums[owned : 2 * owned].astype(BF16)
    far = sums[2 * owned : 2 * owned + n_far].astype(BF16)
    own_ref[...] = own
    recv_sums_ref[...] = recv
    far_ref[...] = far
    away_ref[keep_ref.shape[0] :] = far[n_far // 2 :]
    shape = (n_far, count * HALO_ROWS)
    column = lax.broadcasted_iota(jnp.int32, shape, 1)
    device = column // HALO_ROWS
    there = (column % HALO_ROWS < slot) & (
        block_of(device) + column % HALO_ROWS == lax.broadcasted_iota(jnp.int32, shape, 0)
    )
    halo = mm(jnp.where(there, 1.0, 0.0).astype(BF16), halo_ref[...]).astype(BF16)
    nodes = nodes_ref[...]
    for start in range(0, width, TILE):
        cols = slice(start, start + TILE)
        grads_eo[cols] = mm_rows(zeta_ref[:half, cols], dye1_ref[...]) + mm_rows(zeta_ref[half:, cols], dye2_ref[...])
        grads_ei[cols] = mm_rows(edges1_ref[:, cols], da1_ref[...]) + mm_rows(edges2_ref[:, cols], da2_ref[...])
    grads_ei[width : 2 * width] = mm_rows(nodes, own) + mm_rows(halo, far)
    grads_ei[2 * width :] = mm_rows(nodes, recv)
    put_blocks((grads_eo, grads_ei), me, count, keep_ref, away_ref)


def ride_kernel(step, count, slot, keep_ref, arrived_ref, far_ref, next_keep_ref, next_away_ref, next_far_ref):
    size, half = keep_ref.shape[0], next_keep_ref.shape[0]
    next_keep_ref[...] = keep_ref[:half] + arrived_ref[:half]
    next_away_ref[:half] = keep_ref[half:] + arrived_ref[half:size]
    far = swap_rows(step, count, slot, far_ref[...], arrived_ref[size:])
    next_far_ref[...] = far
    next_away_ref[half:] = mm(take_rows(step + 1, count, slot), far).astype(BF16)


def swap_rows(step, count, slot, far, arrived):
    take = take_rows(step, count, slot)
    stays = 1.0 - jnp.sum(take.astype(F32), axis=0, keepdims=True)
    rows = far.shape[0]
    square = lax.broadcasted_iota(jnp.int32, (rows, rows), 0) == lax.broadcasted_iota(jnp.int32, (rows, rows), 1)
    stay = jnp.where(square, stays, 0.0).astype(BF16)
    return (mm(stay, far) + mm_rows(take, arrived)).astype(BF16)


def node_kernel(
    step, count, slot, own_ref, recv_ref, part_ref, w_send_ref, w_recv_ref, far_ref, pick_ref, out_ref, late_pick_ref
):
    take = take_rows(step, count, slot)
    stays = mm_rows(take, jnp.ones((take.shape[0], pick_ref.shape[1]), BF16)) == 0.0
    early_pick = jnp.where(stays, pick_ref[...], jnp.zeros_like(pick_ref[...]))
    late_pick_ref[...] = mm(take, pick_ref[...]).astype(BF16)
    own = own_ref[...].astype(F32) + mm_rows(early_pick, far_ref[...])
    out_ref[...] = (
        part_ref[...] + mm_cols(own.astype(BF16), w_send_ref[...]) + mm_cols(recv_ref[...], w_recv_ref[...])
    )


def last_kernel(keep_ref, arrived_ref, late_pick_ref, node_ref, w_send_ref, first_ref, rest_ref, grad_ref):
    share, rest = first_ref.shape[0], rest_ref.shape[0]
    size = keep_ref.shape[0]
    far = mm_cols(arrived_ref[size:], w_send_ref[...]).astype(BF16)
    total = keep_ref[...].astype(F32) + arrived_ref[:size].astype(F32)
    first_ref[...] = total[:share]
    rest_ref[...] = total[share : share + rest]
    grad_ref[...] = (node_ref[...] + mm_rows(late_pick_ref[...], far)).astype(BF16)


def add_kernel(keep_ref, arrived_ref, next_keep_ref, next_send_ref):
    half = next_keep_ref.shape[0]
    next_send_ref[...] = keep_ref[half:] + arrived_ref[half:]
    next_keep_ref[...] = keep_ref[:half] + arrived_ref[:half]


def total_kernel(kept_ref, came_ref, first_ref, rest_ref):
    share = first_ref.shape[0]
    total = kept_ref[...].astype(F32) + came_ref[...].astype(F32)
    first_ref[...] = total[:share]
    rest_ref[...] = total[share : share + rest_ref.shape[0]]


VMEM = pl.BlockSpec(memory_space=pltpu.VMEM)
HBM = pl.BlockSpec(memory_space=pltpu.HBM)
COST = pl.CostEstimate(flops=1 << 10, bytes_accessed=1 << 10, transcendentals=0)
LARGE_COST = pl.CostEstimate(flops=1 << 10, bytes_accessed=1 << 26, transcendentals=0)


def kernel_call(kernel, name, outs, scratch, args, near=(), far=(), limit=16, cost=COST, out_spec=None):
    specs = [VMEM] * (len(args) + len(near)) + [HBM] * len(far)
    near = [pltpu.with_memory_space_constraint(array, pltpu.VMEM) for array in near]
    far = [pltpu.with_memory_space_constraint(array, pltpu.HBM) for array in far]
    return pl.pallas_call(
        kernel,
        out_shape=tuple(outs),
        in_specs=specs,
        out_specs=(out_spec or VMEM,) * len(outs),
        scratch_shapes=scratch,
        compiler_params=pltpu.CompilerParams(vmem_limit_bytes=limit << 20),
        cost_estimate=cost,
        name=name,
    )(*args, *near, *far)


def in_order(first, then):
    return lax.optimization_barrier((first, then))


def trade(rows):
    return lax.all_to_all(rows, "patch", split_axis=0, concat_axis=0, tiled=True)


def body(
    count,
    nodes,
    edges,
    cot_nodes,
    w_edge_in,
    w_edge_out,
    w_node_in,
    w_node_out,
    send_rows,
    edge_sender,
    edge_receiver,
):
    owned, width = nodes.shape
    n_edges = edges.shape[0]
    slot = send_rows.shape[2]
    share = width // count
    n_halo = count * HALO_ROWS
    sender = edge_sender.reshape(1, -1)
    receiver = edge_receiver.reshape(1, -1)

    def space(*shape, dtype=BF16):
        return pltpu.VMEM(shape, dtype)

    def block_pair(rows, riders=0):
        size = count // 2 * (-(-(rows * share) // 16) * 16)
        return [space(size, width), space(size + riders, width)]

    n_far = count * slot
    pick, halo_out = kernel_call(
        functools.partial(pick_kernel, count),
        "pick",
        [jax.ShapeDtypeStruct((n_far, owned), BF16), jax.ShapeDtypeStruct((n_halo, width), BF16)],
        [],
        (send_rows[0].T, nodes),
        limit=60,
    )
    halo = trade(halo_out)
    rows, square, ids = space(n_edges, width), space(width, width), space(1, n_edges, dtype=jnp.int32)
    half_rows = space(n_edges // 2, width)
    near = kernel_call(
        local_kernel,
        "local",
        [space(owned, width), square, square, square, space(2 * owned, width), half_rows],
        [square, pltpu.SemaphoreType.DMA((6,))],
        (),
        far=(nodes, w_edge_in, w_edge_out, edges),
    )
    near_nodes, w_send, _, near_out, _, edges1 = near
    keep1, away1, zeta, slope, normed, inv, dagg, node_part, edges2, w_recv, sender, receiver = kernel_call(
        functools.partial(forward_kernel, count, slot),
        "forward",
        block_pair(3)
        + [rows, rows, rows, space(n_edges, 1, dtype=F32)]
        + [space(owned, width), space(owned, width, dtype=F32), half_rows, square, ids, ids],
        [space(2 * width, width), square, space(owned, width), space(2 * owned + n_halo, width)]
        + [space(r, width, dtype=F32) for r in (owned, width, 2 * width)]
        + [pltpu.SemaphoreType.DMA((7,))],
        (halo,),
        near=near,
        far=(edges, sender, receiver, w_node_in, w_node_out, cot_nodes, w_edge_in),
        limit=36,
    )

    def add(keep, arrived):
        half = [space(keep.shape[0] // 2, width)] * 2
        return kernel_call(add_kernel, "add", half, [], (keep, arrived), limit=8, cost=LARGE_COST)

    def ride(step, keep, arrived, far):
        half = keep.shape[0] // 2
        outs = [space(half, width), space(half + n_far // 2, width), space(n_far, width)]
        kernel = functools.partial(ride_kernel, step, count, slot)
        return kernel_call(kernel, "ride", outs, [], (keep, arrived, far), limit=8)

    came1 = cube_permute(away1, 0, count)
    halves = [half_rows] * 2
    args = (receiver, zeta, slope, normed, inv, dagg, near_out)
    dye1, da1 = kernel_call(functools.partial(backward_kernel, 0), "backward", halves, [], (), args)
    came1, dye1 = in_order(came1, dye1)
    keep1, away1 = add(keep1, came1)
    away1, dagg = in_order(away1, dagg)
    came1 = cube_permute(away1, 1, count)
    args = (receiver, zeta, slope, normed, inv, dagg, near_out)
    dye2, da2 = kernel_call(functools.partial(backward_kernel, n_edges // 2), "backward", halves, [], (), args)
    keep2, away2, own_sums, recv_sums, far_sums = kernel_call(
        functools.partial(weights_kernel, count, slot),
        "weights",
        block_pair(4, n_far // 2) + [space(owned, width), space(owned, width), space(n_far, width)],
        [space(r, width, dtype=F32) for r in (2 * owned + -(-n_far // LANES) * LANES, width, 3 * width)],
        (halo,),
        (sender, receiver, near_nodes, edges1, edges2, zeta, dye1, dye2, da1, da2),
    )
    steps = count.bit_length() - 1
    for step in range(1, steps - 1):
        keep1, away1 = add(keep1, came1)
        if step == 1:
            away1, away2 = in_order(away1, away2)
            came2 = cube_permute(away2, 0, count)
        else:
            away1, came2 = in_order(away1, came2)
        came1 = cube_permute(away1, step + 1, count)
        keep2, away2, far_sums = ride(step - 1, keep2, came2, far_sums)
        came2 = cube_permute(away2, step, count)
    keep2, away2, far_sums = ride(steps - 2, keep2, came2, far_sums)
    came1, away2 = in_order(came1, away2)
    _, (da1, da2, own_sums) = in_order(away2, (da1, da2, own_sums))
    came2 = cube_permute(away2, steps - 1, count)
    edge_grad = mm_cols(jnp.concatenate([da1, da2]), w_edge_in[:width]).astype(BF16)
    node_sum, late_pick = kernel_call(
        functools.partial(node_kernel, steps - 1, count, slot),
        "node",
        [space(owned, width, dtype=F32), space(n_far // 2, owned)],
        [],
        (own_sums, recv_sums, node_part, w_send, w_recv, far_sums, pick),
    )

    def whole(*parts):
        return [jax.ShapeDtypeStruct((part * share, width), F32) for part in parts]

    node_out, node_in = kernel_call(total_kernel, "node_total", whole(1, 2), [], (keep1, came1), limit=8)
    edge_out, edge_in, node_grad = kernel_call(
        last_kernel,
        "last",
        whole(1, 3) + [jax.ShapeDtypeStruct((owned, width), BF16)],
        [],
        (keep2, came2, late_pick, node_sum, w_send),
        limit=8,
    )
    return node_grad, edge_grad, edge_in, edge_out, node_in, node_out


def solution(mesh):
    rows = P(("groups", "patch"), None)
    flat = P(("groups", "patch"))
    return jax.shard_map(
        functools.partial(body, mesh.shape["patch"]),
        mesh=mesh,
        in_specs=(rows, rows, rows, P(), P(), P(), P(), P(("groups", "patch"), None, None), flat, flat),
        out_specs=(rows,) * 6,
        check_vma=False,
    )
```

```python
import functools

import jax
import jax.numpy as jnp
from jax import lax
from jax.experimental import pallas as pl
from jax.experimental.pallas import tpu as pltpu
from jax.sharding import PartitionSpec as P

BF16 = jnp.bfloat16
F32 = jnp.float32
EPS = 1e-05
LANES = 128
TILE = 256
HALO_ROWS = 8


def mm(left, right):
    return jnp.dot(left, right, preferred_element_type=F32)


def mm_rows(left, right):
    return lax.dot_general(left, right, (((0,), (0,)), ((), ())), preferred_element_type=F32)


def mm_cols(left, right):
    return lax.dot_general(left, right, (((1,), (1,)), ((), ())), preferred_element_type=F32)


def sigmoid(values):
    return 0.5 * jnp.tanh(0.5 * values) + 0.5


def normalize(values):
    center = values - jnp.mean(values, axis=-1, keepdims=True)
    inv_std = lax.rsqrt(jnp.mean(center * center, axis=-1, keepdims=True) + EPS)
    return center * inv_std, inv_std


def norm_back(upstream, normed, inv_std):
    return inv_std * (
        upstream
        - jnp.mean(upstream, axis=-1, keepdims=True)
        - normed * jnp.mean(upstream * normed, axis=-1, keepdims=True)
    )


def cube_masks(count):
    return [1 << i for i in range(count.bit_length() - 1)]


def cube_orders(count):
    rest = list(range(1, count.bit_length() - 1))
    return [0] + rest, [0] + rest[:2][::-1] + rest[2:]


def cube_place(apart, parity, count):
    bits = count.bit_length() - 1
    coords = [(apart >> i) & 1 for i in range(bits)]
    even, odd = [sum(coords[dim] << (bits - 1 - j) for j, dim in enumerate(order)) for order in cube_orders(count)]
    return jnp.where(parity == 0, even, odd)


def cube_permute(blocks, step, count):
    mask, orders = cube_masks(count), cube_orders(count)
    pairs = [(i, i ^ mask[orders[i & 1][step]]) for i in range(count)]
    return lax.ppermute(blocks, "patch", pairs)


def one_hot_cols(ids, width):
    rows = ids.shape[1]
    spread = jnp.transpose(jnp.broadcast_to(ids, (LANES, rows)))
    lane = lax.broadcasted_iota(jnp.int32, (rows, LANES), 1)
    tiles = [jnp.where(spread == lane + start, 1.0, 0.0).astype(BF16) for start in range(0, width, LANES)]
    return jnp.concatenate(tiles, axis=1)[:, :width]


def hot_cols(first, second, width):
    rows = first.shape[1]
    left = jnp.transpose(jnp.broadcast_to(first, (LANES, rows)))
    right = jnp.transpose(jnp.broadcast_to(second, (LANES, rows)))
    lane = lax.broadcasted_iota(jnp.int32, (rows, LANES), 1)
    tiles = [
        jnp.where((left == lane + start) | (right == lane + start), 1.0, 0.0).astype(BF16)
        for start in range(0, width, LANES)
    ]
    return jnp.concatenate(tiles, axis=1)


def hot_rows(first, second, width):
    row = lax.broadcasted_iota(jnp.int32, (width, first.shape[1]), 0)
    return jnp.where((row == first) | (row == second), 1.0, 0.0).astype(BF16)


def edge_ids(rows, owned, slot, send_ref, recv_ref, block_of):
    sender = send_ref[:, rows]
    receiver = recv_ref[:, rows]
    far = sender - owned
    sender = jnp.where(far < 0, sender, 2 * owned + block_of(far // slot) + far % slot)
    return sender, jnp.maximum(receiver, 0) + owned, receiver


def take_rows(step, count, slot):
    weight = count >> (step + 1)
    shape = (count // 2 * slot, count * slot)
    out = lax.broadcasted_iota(jnp.int32, shape, 0)
    block, row = out // slot, out % slot
    place = block // weight * 2 * weight + weight + block % weight
    return jnp.where(lax.broadcasted_iota(jnp.int32, shape, 1) == place * slot + row, 1.0, 0.0).astype(BF16)


def put_blocks(sources, me, count, keep_ref, send_ref):
    shares = [source.shape[0] // count for source in sources]
    half = count // 2
    size = keep_ref.shape[0] // half
    spare = size - sum(shares)
    bits = count.bit_length() - 1
    for place in range(count):
        apart = [
            sum(((place >> (bits - 1 - j)) & 1) << dim for j, dim in enumerate(order)) for order in cube_orders(count)
        ]
        odd_target = (me ^ (place // half)) & 1
        target = me ^ jnp.where(odd_target == 0, *apart)
        parts = [
            source[pl.ds(pl.multiple_of(target * share, share), share)] for source, share in zip(sources, shares)
        ]
        if spare:
            parts.append(jnp.zeros((spare, keep_ref.shape[1]), F32))
        start = place % half * size
        (keep_ref if place < half else send_ref)[start : start + size] = jnp.concatenate(parts, axis=0).astype(BF16)


def pick_kernel(count, picks_ref, nodes_ref, pick_ref, rows_ref):
    slot = picks_ref.shape[0]
    owned = nodes_ref.shape[0]
    me = lax.axis_index("patch")

    def choose(rows, start):
        shape = (rows, count)
        row = lax.broadcasted_iota(jnp.int32, shape, 0)
        first = start(lax.broadcasted_iota(jnp.int32, shape, 1))
        ids = jnp.zeros(shape, jnp.int32)
        for place in range(slot):
            ids = ids + jnp.where(row == first + place, picks_ref[place : place + 1] + 1, 0)
        ids = jnp.sum(ids.astype(F32), axis=1, keepdims=True).astype(jnp.int32) - 1
        node = lax.broadcasted_iota(jnp.int32, (rows, owned), 1)
        return jnp.where(node == ids, 1.0, 0.0).astype(BF16)

    rows_ref[...] = mm(choose(count * HALO_ROWS, lambda device: device * HALO_ROWS), nodes_ref[...]).astype(BF16)
    pick_ref[...] = choose(count * slot, lambda device: cube_place(device ^ me, me & 1, count) * slot)


def local_kernel(
    count,
    slot,
    nodes_far,
    w_edge_in_far,
    w_edge_out_far,
    edges_far,
    nodes_ref,
    w_send,
    w_edge_out_ref,
    table,
    edges1_ref,
    moves_ref,
    w_recv,
    sems,
):
    owned, width = nodes_ref.shape
    pairs = (
        (nodes_far, nodes_ref),
        (w_edge_in_far.at[width : 2 * width], w_send),
        (w_edge_in_far.at[2 * width :], w_recv),
        (w_edge_in_far.at[:width], table.at[:width]),
        (w_edge_out_far, w_edge_out_ref),
        (edges_far.at[: edges1_ref.shape[0]], edges1_ref),
    )
    copies = [pltpu.make_async_copy(src, dst, sems.at[i]) for i, (src, dst) in enumerate(pairs)]
    for copy in copies:
        copy.start()
    for step in range(moves_ref.shape[0]):
        moves_ref[step] = move_rows(step, count, slot)
    copies[0].wait()
    nodes = nodes_ref[...]
    copies[1].wait()
    table[width : width + owned] = mm(nodes, w_send[...]).astype(BF16)
    copies[2].wait()
    table[width + owned :] = mm(nodes, w_recv[...]).astype(BF16)
    for copy in copies[3:]:
        copy.wait()


def forward_kernel(
    count,
    slot,
    halo_ref,
    nodes_ref,
    w_send,
    w_edge_out_ref,
    own_table,
    edges1_ref,
    edges_far,
    send_far,
    recv_far,
    w_node_in_far,
    w_node_out_far,
    cot_far,
    w_edge_in_far,
    keep_ref,
    away_ref,
    zeta_ref,
    slope_ref,
    normed_ref,
    inv_ref,
    dagg_ref,
    node_part_ref,
    edges2_ref,
    w_recv,
    send_ref,
    recv_ref,
    w_node_in_ref,
    w_node_out_ref,
    cot_ref,
    table,
    agg,
    grads_no,
    grads_ni,
    sems,
):
    owned, width = nodes_ref.shape
    n_table = table.shape[0]
    half = edges1_ref.shape[0]
    pairs = (
        (send_far, send_ref),
        (recv_far, recv_ref),
        (edges_far.at[half:], edges2_ref),
        (w_node_in_far, w_node_in_ref),
        (w_node_out_far, w_node_out_ref),
        (cot_far, cot_ref),
        (w_edge_in_far.at[2 * width :], w_recv),
    )
    copies = [pltpu.make_async_copy(src, dst, sems.at[i]) for i, (src, dst) in enumerate(pairs)]
    for copy in copies:
        copy.start()
    nodes = nodes_ref[...]
    table[: width + 2 * owned] = own_table[...]
    table[width + 2 * owned :] = mm(halo_ref[...], w_send[...]).astype(BF16)
    for copy in copies[:2]:
        copy.wait()
    for part, edges_ref in enumerate((edges1_ref, edges2_ref)):
        if part:
            copies[2].wait()
        rows = slice(part * half, (part + 1) * half)
        sender, safe, receiver = edge_ids(rows, owned, slot, send_ref, recv_ref, lambda device: device * HALO_ROWS)
        hot = hot_cols(sender, safe, n_table - width)
        pre = mm(jnp.concatenate([edges_ref[...], hot], axis=1), table[...])
        sigma = sigmoid(pre)
        zed = (pre * sigma).astype(BF16)
        zeta_ref[rows] = zed
        slope_ref[rows] = (sigma * (1.0 + pre * (1.0 - sigma))).astype(BF16)
        unit, inv_std = normalize(mm(zed, w_edge_out_ref[...]))
        message = unit.astype(BF16)
        normed_ref[rows] = message
        inv_ref[rows] = inv_std
        gathered = mm(hot_rows(receiver, receiver, owned), message)
        agg[...] = agg[...] + gathered if part else gathered

    for copy in copies[3:]:
        copy.wait()
    inbox = agg[...].astype(BF16)
    pre = mm(nodes, w_node_in_ref[:width]) + mm(inbox, w_node_in_ref[width:])
    sigma = sigmoid(pre)
    zed = (pre * sigma).astype(BF16)
    unit, inv_std = normalize(mm(zed, w_node_out_ref[...]))
    upstream = cot_ref[...].astype(F32)
    dy = norm_back(upstream, unit, inv_std).astype(BF16)
    db = (mm_cols(dy, w_node_out_ref[...]) * (sigma * (1.0 + pre * (1.0 - sigma)))).astype(BF16)
    dagg_ref[...] = mm_cols(db, w_node_in_ref[width:]).astype(BF16)
    node_part_ref[...] = upstream + mm_cols(db, w_node_in_ref[:width])
    grads_no[...] = mm_rows(zed, dy)
    grads_ni[:width] = mm_rows(nodes, db)
    grads_ni[width:] = mm_rows(inbox, db)
    put_blocks((grads_no, grads_ni), lax.axis_index("patch"), count, keep_ref, away_ref)


def backward_kernel(
    first, recv_ref, zeta_ref, slope_ref, normed_ref, inv_ref, dagg_ref, w_edge_out_ref, dye_ref, da_ref
):
    rows = slice(first, first + dye_ref.shape[0])
    up = mm(one_hot_cols(recv_ref[:, rows], dagg_ref.shape[0]), dagg_ref[...])
    dye = norm_back(up, normed_ref[rows].astype(F32), inv_ref[rows]).astype(BF16)
    dye_ref[...] = dye
    da_ref[...] = (mm_cols(dye, w_edge_out_ref[...]) * slope_ref[rows].astype(F32)).astype(BF16)


def weights_kernel(
    count,
    slot,
    halo_ref,
    send_ref,
    recv_ref,
    nodes_ref,
    edges1_ref,
    edges2_ref,
    zeta_ref,
    dye1_ref,
    dye2_ref,
    da1_ref,
    da2_ref,
    keep_ref,
    away_ref,
    own_ref,
    recv_sums_ref,
    far_ref,
    sums,
    grads_eo,
    grads_ei,
):
    owned, width = nodes_ref.shape
    n_table = sums.shape[0]
    n_far = count * slot
    me = lax.axis_index("patch")

    def block_of(device):
        return cube_place(device ^ me, device & 1, count) * slot

    half = da1_ref.shape[0]
    sender, safe, _ = edge_ids(slice(None), owned, slot, send_ref, recv_ref, block_of)
    hot = hot_rows(sender, safe, n_table)
    sums[...] = mm(hot[:, :half], da1_ref[...]) + mm(hot[:, half:], da2_ref[...])

    own = sums[:owned].astype(BF16)
    recv = sums[owned : 2 * owned].astype(BF16)
    far = sums[2 * owned : 2 * owned + n_far].astype(BF16)
    own_ref[...] = own
    recv_sums_ref[...] = recv
    far_ref[...] = far
    away_ref[keep_ref.shape[0] :] = far[n_far // 2 :]
    shape = (n_far, count * HALO_ROWS)
    column = lax.broadcasted_iota(jnp.int32, shape, 1)
    device = column // HALO_ROWS
    there = (column % HALO_ROWS < slot) & (
        block_of(device) + column % HALO_ROWS == lax.broadcasted_iota(jnp.int32, shape, 0)
    )
    halo = mm(jnp.where(there, 1.0, 0.0).astype(BF16), halo_ref[...]).astype(BF16)
    nodes = nodes_ref[...]
    for start in range(0, width, TILE):
        cols = slice(start, start + TILE)
        grads_eo[cols] = mm_rows(zeta_ref[:half, cols], dye1_ref[...]) + mm_rows(zeta_ref[half:, cols], dye2_ref[...])
        grads_ei[cols] = mm_rows(edges1_ref[:, cols], da1_ref[...]) + mm_rows(edges2_ref[:, cols], da2_ref[...])
    grads_ei[width : 2 * width] = mm_rows(nodes, own) + mm_rows(halo, far)
    grads_ei[2 * width :] = mm_rows(nodes, recv)
    put_blocks((grads_eo, grads_ei), me, count, keep_ref, away_ref)


def move_rows(step, count, slot):
    take = take_rows(step, count, slot)
    rows = take.shape[1]
    square = lax.broadcasted_iota(jnp.int32, (rows, rows), 0) == lax.broadcasted_iota(jnp.int32, (rows, rows), 1)
    eye = jnp.where(square, 1.0, 0.0)
    stay = (eye - mm_rows(take, take)).astype(BF16)
    small = eye[: rows // 2, : rows // 2].astype(BF16)
    after = jnp.concatenate([stay, mm_rows(take, small).astype(BF16)], axis=1)
    return jnp.concatenate([mm(take_rows(step + 1, count, slot), after).astype(BF16), after], axis=0)


def ride_kernel(step, keep_ref, arrived_ref, far_ref, moves_ref, next_keep_ref, next_away_ref, next_far_ref):
    size, half = keep_ref.shape[0], next_keep_ref.shape[0]
    moved = mm(moves_ref[step], jnp.concatenate([far_ref[...], arrived_ref[size:]], axis=0)).astype(BF16)
    next_keep_ref[...] = keep_ref[:half] + arrived_ref[:half]
    next_away_ref[:half] = keep_ref[half:] + arrived_ref[half:size]
    split = moved.shape[0] - next_far_ref.shape[0]
    next_away_ref[half:] = moved[:split]
    next_far_ref[...] = moved[split:]


def node_kernel(
    step, count, slot, own_ref, recv_ref, part_ref, w_send_ref, w_recv_ref, far_ref, pick_ref, out_ref, late_pick_ref
):
    take = take_rows(step, count, slot)
    stays = mm_rows(take, jnp.ones((take.shape[0], pick_ref.shape[1]), BF16)) == 0.0
    early_pick = jnp.where(stays, pick_ref[...], jnp.zeros_like(pick_ref[...]))
    late_pick_ref[...] = mm(take, pick_ref[...]).astype(BF16)
    own = own_ref[...].astype(F32) + mm_rows(early_pick, far_ref[...])
    out_ref[...] = (
        part_ref[...] + mm_cols(own.astype(BF16), w_send_ref[...]) + mm_cols(recv_ref[...], w_recv_ref[...])
    )


def last_kernel(keep_ref, arrived_ref, late_pick_ref, node_ref, w_send_ref, first_ref, rest_ref, grad_ref):
    share, rest = first_ref.shape[0], rest_ref.shape[0]
    size = keep_ref.shape[0]
    far = mm_cols(arrived_ref[size:], w_send_ref[...]).astype(BF16)
    total = keep_ref[...].astype(F32) + arrived_ref[:size].astype(F32)
    first_ref[...] = total[:share]
    rest_ref[...] = total[share : share + rest]
    grad_ref[...] = (node_ref[...] + mm_rows(late_pick_ref[...], far)).astype(BF16)


def add_kernel(keep_ref, arrived_ref, next_keep_ref, next_send_ref):
    half = next_keep_ref.shape[0]
    next_send_ref[...] = keep_ref[half:] + arrived_ref[half:]
    next_keep_ref[...] = keep_ref[:half] + arrived_ref[:half]


def total_kernel(kept_ref, came_ref, first_ref, rest_ref):
    share = first_ref.shape[0]
    total = kept_ref[...].astype(F32) + came_ref[...].astype(F32)
    first_ref[...] = total[:share]
    rest_ref[...] = total[share : share + rest_ref.shape[0]]


VMEM = pl.BlockSpec(memory_space=pltpu.VMEM)
HBM = pl.BlockSpec(memory_space=pltpu.HBM)
COST = pl.CostEstimate(flops=1 << 10, bytes_accessed=1 << 10, transcendentals=0)
LARGE_COST = pl.CostEstimate(flops=1 << 10, bytes_accessed=1 << 26, transcendentals=0)


def kernel_call(kernel, name, outs, scratch, args, near=(), far=(), limit=16, cost=COST, out_spec=None):
    specs = [VMEM] * (len(args) + len(near)) + [HBM] * len(far)
    near = [pltpu.with_memory_space_constraint(array, pltpu.VMEM) for array in near]
    far = [pltpu.with_memory_space_constraint(array, pltpu.HBM) for array in far]
    return pl.pallas_call(
        kernel,
        out_shape=tuple(outs),
        in_specs=specs,
        out_specs=(out_spec or VMEM,) * len(outs),
        scratch_shapes=scratch,
        compiler_params=pltpu.CompilerParams(vmem_limit_bytes=limit << 20),
        cost_estimate=cost,
        name=name,
    )(*args, *near, *far)


def in_order(first, then):
    return lax.optimization_barrier((first, then))


def trade(rows):
    return lax.all_to_all(rows, "patch", split_axis=0, concat_axis=0, tiled=True)


def body(
    count,
    nodes,
    edges,
    cot_nodes,
    w_edge_in,
    w_edge_out,
    w_node_in,
    w_node_out,
    send_rows,
    edge_sender,
    edge_receiver,
):
    owned, width = nodes.shape
    n_edges = edges.shape[0]
    slot = send_rows.shape[2]
    share = width // count
    n_halo = count * HALO_ROWS
    sender = edge_sender.reshape(1, -1)
    receiver = edge_receiver.reshape(1, -1)

    def space(*shape, dtype=BF16):
        return pltpu.VMEM(shape, dtype)

    def block_pair(rows, riders=0):
        size = count // 2 * (-(-(rows * share) // 16) * 16)
        return [space(size, width), space(size + riders, width)]

    n_far = count * slot
    steps = count.bit_length() - 1
    pick, halo_out = kernel_call(
        functools.partial(pick_kernel, count),
        "pick",
        [jax.ShapeDtypeStruct((n_far, owned), BF16), jax.ShapeDtypeStruct((n_halo, width), BF16)],
        [],
        (send_rows[0].T, nodes),
        limit=60,
    )
    halo = trade(halo_out)
    rows, square, ids = space(n_edges, width), space(width, width), space(1, n_edges, dtype=jnp.int32)
    half_rows = space(n_edges // 2, width)
    *near, moves = kernel_call(
        functools.partial(local_kernel, count, slot),
        "local",
        [space(owned, width), square, square, space(width + 2 * owned, width), half_rows]
        + [space(steps - 1, n_far * 3 // 2, n_far * 3 // 2)],
        [square, pltpu.SemaphoreType.DMA((6,))],
        (),
        far=(nodes, w_edge_in, w_edge_out, edges),
    )
    near_nodes, w_send, near_out, _, edges1 = near
    keep1, away1, zeta, slope, normed, inv, dagg, node_part, edges2, w_recv, sender, receiver = kernel_call(
        functools.partial(forward_kernel, count, slot),
        "forward",
        block_pair(3)
        + [rows, rows, rows, space(n_edges, 1, dtype=F32)]
        + [space(owned, width), space(owned, width, dtype=F32), half_rows, square, ids, ids],
        [space(2 * width, width), square, space(owned, width), space(width + 2 * owned + n_halo, width)]
        + [space(r, width, dtype=F32) for r in (owned, width, 2 * width)]
        + [pltpu.SemaphoreType.DMA((7,))],
        (halo,),
        near=near,
        far=(edges, sender, receiver, w_node_in, w_node_out, cot_nodes, w_edge_in),
        limit=36,
    )

    def add(keep, arrived):
        half = [space(keep.shape[0] // 2, width)] * 2
        return kernel_call(add_kernel, "add", half, [], (keep, arrived), limit=8, cost=LARGE_COST)

    def ride(step, keep, arrived, far):
        half = keep.shape[0] // 2
        outs = [space(half, width), space(half + n_far // 2, width), space(n_far, width)]
        return kernel_call(
            functools.partial(ride_kernel, step), "ride", outs, [], (keep, arrived, far), (moves,), limit=8
        )

    came1 = cube_permute(away1, 0, count)
    halves = [half_rows] * 2
    args = (receiver, zeta, slope, normed, inv, dagg, near_out)
    dye1, da1 = kernel_call(functools.partial(backward_kernel, 0), "backward", halves, [], (), args)
    came1, dye1 = in_order(came1, dye1)
    keep1, away1 = add(keep1, came1)
    away1, dagg = in_order(away1, dagg)
    came1 = cube_permute(away1, 1, count)
    args = (receiver, zeta, slope, normed, inv, dagg, near_out)
    dye2, da2 = kernel_call(functools.partial(backward_kernel, n_edges // 2), "backward", halves, [], (), args)
    keep2, away2, own_sums, recv_sums, far_sums = kernel_call(
        functools.partial(weights_kernel, count, slot),
        "weights",
        block_pair(4, n_far // 2) + [space(owned, width), space(owned, width), space(n_far, width)],
        [space(r, width, dtype=F32) for r in (2 * owned + -(-n_far // LANES) * LANES, width, 3 * width)],
        (halo,),
        (sender, receiver, near_nodes, edges1, edges2, zeta, dye1, dye2, da1, da2),
    )
    for step in range(1, steps - 1):
        keep1, away1 = add(keep1, came1)
        if step == 1:
            away1, away2 = in_order(away1, away2)
            came2 = cube_permute(away2, 0, count)
        else:
            away1, came2 = in_order(away1, came2)
        came1 = cube_permute(away1, step + 1, count)
        keep2, away2, far_sums = ride(step - 1, keep2, came2, far_sums)
        came2 = cube_permute(away2, step, count)
    keep2, away2, far_sums = ride(steps - 2, keep2, came2, far_sums)
    came1, away2 = in_order(came1, away2)
    _, (da1, da2, own_sums) = in_order(away2, (da1, da2, own_sums))
    came2 = cube_permute(away2, steps - 1, count)
    edge_grad = mm_cols(jnp.concatenate([da1, da2]), w_edge_in[:width]).astype(BF16)
    node_sum, late_pick = kernel_call(
        functools.partial(node_kernel, steps - 1, count, slot),
        "node",
        [space(owned, width, dtype=F32), space(n_far // 2, owned)],
        [],
        (own_sums, recv_sums, node_part, w_send, w_recv, far_sums, pick),
    )

    def whole(*parts):
        return [jax.ShapeDtypeStruct((part * share, width), F32) for part in parts]

    node_out, node_in = kernel_call(total_kernel, "node_total", whole(1, 2), [], (keep1, came1), limit=8)
    edge_out, edge_in, node_grad = kernel_call(
        last_kernel,
        "last",
        whole(1, 3) + [jax.ShapeDtypeStruct((owned, width), BF16)],
        [],
        (keep2, came2, late_pick, node_sum, w_send),
        limit=8,
    )
    return node_grad, edge_grad, edge_in, edge_out, node_in, node_out


def solution(mesh):
    rows = P(("groups", "patch"), None)
    flat = P(("groups", "patch"))
    return jax.shard_map(
        functools.partial(body, mesh.shape["patch"]),
        mesh=mesh,
        in_specs=(rows, rows, rows, P(), P(), P(), P(), P(("groups", "patch"), None, None), flat, flat),
        out_specs=(rows,) * 6,
        check_vma=False,
    )
```

```python
import functools

import jax
import jax.numpy as jnp
from jax import lax
from jax.experimental import pallas as pl
from jax.experimental.pallas import tpu as pltpu
from jax.sharding import PartitionSpec as P

BF16 = jnp.bfloat16
F32 = jnp.float32
EPS = 1e-05
LANES = 128
TILE = 256
HALO_ROWS = 8


def mm(left, right):
    return jnp.dot(left, right, preferred_element_type=F32)


def mm_rows(left, right):
    return lax.dot_general(left, right, (((0,), (0,)), ((), ())), preferred_element_type=F32)


def mm_cols(left, right):
    return lax.dot_general(left, right, (((1,), (1,)), ((), ())), preferred_element_type=F32)


def sigmoid(values):
    return 0.5 * jnp.tanh(0.5 * values) + 0.5


def normalize(values):
    center = values - jnp.mean(values, axis=-1, keepdims=True)
    inv_std = lax.rsqrt(jnp.mean(center * center, axis=-1, keepdims=True) + EPS)
    return center * inv_std, inv_std


def norm_back(upstream, normed, inv_std):
    return inv_std * (
        upstream
        - jnp.mean(upstream, axis=-1, keepdims=True)
        - normed * jnp.mean(upstream * normed, axis=-1, keepdims=True)
    )


def cube_masks(count):
    return [1 << i for i in range(count.bit_length() - 1)]


def cube_orders(count):
    rest = list(range(1, count.bit_length() - 1))
    return [0] + rest, [0] + rest[:2][::-1] + rest[2:]


def cube_place(apart, parity, count):
    bits = count.bit_length() - 1
    coords = [(apart >> i) & 1 for i in range(bits)]
    even, odd = [sum(coords[dim] << (bits - 1 - j) for j, dim in enumerate(order)) for order in cube_orders(count)]
    return jnp.where(parity == 0, even, odd)


def cube_permute(blocks, step, count):
    mask, orders = cube_masks(count), cube_orders(count)
    pairs = [(i, i ^ mask[orders[i & 1][step]]) for i in range(count)]
    return lax.ppermute(blocks, "patch", pairs)


def one_hot_cols(ids, width):
    rows = ids.shape[1]
    spread = jnp.transpose(jnp.broadcast_to(ids, (LANES, rows)))
    lane = lax.broadcasted_iota(jnp.int32, (rows, LANES), 1)
    tiles = [jnp.where(spread == lane + start, 1.0, 0.0).astype(BF16) for start in range(0, width, LANES)]
    return jnp.concatenate(tiles, axis=1)[:, :width]


def hot_cols(first, second, width):
    rows = first.shape[1]
    left = jnp.transpose(jnp.broadcast_to(first, (LANES, rows)))
    right = jnp.transpose(jnp.broadcast_to(second, (LANES, rows)))
    lane = lax.broadcasted_iota(jnp.int32, (rows, LANES), 1)
    tiles = [
        jnp.where((left == lane + start) | (right == lane + start), 1.0, 0.0).astype(BF16)
        for start in range(0, width, LANES)
    ]
    return jnp.concatenate(tiles, axis=1)


def hot_rows(first, second, width):
    row = lax.broadcasted_iota(jnp.int32, (width, first.shape[1]), 0)
    return jnp.where((row == first) | (row == second), 1.0, 0.0).astype(BF16)


def edge_ids(rows, owned, slot, send_ref, recv_ref, block_of):
    sender = send_ref[:, rows]
    receiver = recv_ref[:, rows]
    far = sender - owned
    sender = jnp.where(far < 0, sender, 2 * owned + block_of(far // slot) + far % slot)
    return sender, jnp.maximum(receiver, 0) + owned, receiver


def take_rows(step, count, slot):
    weight = count >> (step + 1)
    shape = (count // 2 * slot, count * slot)
    out = lax.broadcasted_iota(jnp.int32, shape, 0)
    block, row = out // slot, out % slot
    place = block // weight * 2 * weight + weight + block % weight
    return jnp.where(lax.broadcasted_iota(jnp.int32, shape, 1) == place * slot + row, 1.0, 0.0).astype(BF16)


def put_blocks(sources, me, count, keep_ref, *send_refs):
    shares = [source.shape[0] // count for source in sources]
    half = count // 2
    size = keep_ref.shape[0] // half
    spare = size - sum(shares)
    bits = count.bit_length() - 1
    for place in range(count):
        apart = [
            sum(((place >> (bits - 1 - j)) & 1) << dim for j, dim in enumerate(order)) for order in cube_orders(count)
        ]
        odd_target = (me ^ (place // half)) & 1
        target = me ^ jnp.where(odd_target == 0, *apart)
        parts = [
            source[pl.ds(pl.multiple_of(target * share, share), share)] for source, share in zip(sources, shares)
        ]
        if spare:
            parts.append(jnp.zeros((spare, keep_ref.shape[1]), F32))
        each = half // len(send_refs)
        ref = keep_ref if place < half else send_refs[(place - half) // each]
        start = (place if place < half else place % each) * size
        ref[start : start + size] = jnp.concatenate(parts, axis=0).astype(BF16)


def pick_kernel(count, picks_ref, nodes_ref, pick_ref, rows_ref):
    slot = picks_ref.shape[0]
    owned = nodes_ref.shape[0]
    me = lax.axis_index("patch")

    def choose(rows, start):
        shape = (rows, count)
        row = lax.broadcasted_iota(jnp.int32, shape, 0)
        first = start(lax.broadcasted_iota(jnp.int32, shape, 1))
        ids = jnp.zeros(shape, jnp.int32)
        for place in range(slot):
            ids = ids + jnp.where(row == first + place, picks_ref[place : place + 1] + 1, 0)
        ids = jnp.sum(ids.astype(F32), axis=1, keepdims=True).astype(jnp.int32) - 1
        node = lax.broadcasted_iota(jnp.int32, (rows, owned), 1)
        return jnp.where(node == ids, 1.0, 0.0).astype(BF16)

    rows_ref[...] = mm(choose(count * HALO_ROWS, lambda device: device * HALO_ROWS), nodes_ref[...]).astype(BF16)
    pick_ref[...] = choose(count * slot, lambda device: cube_place(device ^ me, me & 1, count) * slot)


def local_kernel(
    count,
    slot,
    nodes_far,
    w_edge_in_far,
    w_edge_out_far,
    edges_far,
    nodes_ref,
    w_send,
    w_edge_out_ref,
    table,
    edges1_ref,
    moves_ref,
    w_recv,
    sems,
):
    owned, width = nodes_ref.shape
    pairs = (
        (nodes_far, nodes_ref),
        (w_edge_in_far.at[width : 2 * width], w_send),
        (w_edge_in_far.at[2 * width :], w_recv),
        (w_edge_in_far.at[:width], table.at[:width]),
        (w_edge_out_far, w_edge_out_ref),
        (edges_far.at[: edges1_ref.shape[0]], edges1_ref),
    )
    copies = [pltpu.make_async_copy(src, dst, sems.at[i]) for i, (src, dst) in enumerate(pairs)]
    for copy in copies:
        copy.start()
    for step in range(moves_ref.shape[0]):
        moves_ref[step] = move_rows(step, count, slot)
    copies[0].wait()
    nodes = nodes_ref[...]
    copies[1].wait()
    table[width : width + owned] = mm(nodes, w_send[...]).astype(BF16)
    copies[2].wait()
    table[width + owned :] = mm(nodes, w_recv[...]).astype(BF16)
    for copy in copies[3:]:
        copy.wait()


def forward_kernel(
    count,
    slot,
    halo_ref,
    nodes_ref,
    w_send,
    w_edge_out_ref,
    own_table,
    edges1_ref,
    edges_far,
    send_far,
    recv_far,
    w_node_in_far,
    w_node_out_far,
    cot_far,
    w_edge_in_far,
    keep_ref,
    away_ref,
    zeta_ref,
    slope_ref,
    normed_ref,
    inv_ref,
    dagg_ref,
    node_part_ref,
    edges2_ref,
    w_recv,
    send_ref,
    recv_ref,
    w_node_in_ref,
    w_node_out_ref,
    cot_ref,
    table,
    agg,
    grads_no,
    grads_ni,
    sems,
):
    owned, width = nodes_ref.shape
    n_table = table.shape[0]
    half = edges1_ref.shape[0]
    pairs = (
        (send_far, send_ref),
        (recv_far, recv_ref),
        (edges_far.at[half:], edges2_ref),
        (w_node_in_far, w_node_in_ref),
        (w_node_out_far, w_node_out_ref),
        (cot_far, cot_ref),
        (w_edge_in_far.at[2 * width :], w_recv),
    )
    copies = [pltpu.make_async_copy(src, dst, sems.at[i]) for i, (src, dst) in enumerate(pairs)]
    for copy in copies:
        copy.start()
    nodes = nodes_ref[...]
    table[: width + 2 * owned] = own_table[...]
    table[width + 2 * owned :] = mm(halo_ref[...], w_send[...]).astype(BF16)
    for copy in copies[:2]:
        copy.wait()
    for part, edges_ref in enumerate((edges1_ref, edges2_ref)):
        if part:
            copies[2].wait()
        rows = slice(part * half, (part + 1) * half)
        sender, safe, receiver = edge_ids(rows, owned, slot, send_ref, recv_ref, lambda device: device * HALO_ROWS)
        hot = hot_cols(sender, safe, n_table - width)
        pre = mm(jnp.concatenate([edges_ref[...], hot], axis=1), table[...])
        sigma = sigmoid(pre)
        zed = (pre * sigma).astype(BF16)
        zeta_ref[rows] = zed
        slope_ref[rows] = (sigma * (1.0 + pre * (1.0 - sigma))).astype(BF16)
        unit, inv_std = normalize(mm(zed, w_edge_out_ref[...]))
        message = unit.astype(BF16)
        normed_ref[rows] = message
        inv_ref[rows] = inv_std
        gathered = mm(hot_rows(receiver, receiver, owned), message)
        agg[...] = agg[...] + gathered if part else gathered

    for copy in copies[3:]:
        copy.wait()
    inbox = agg[...].astype(BF16)
    pre = mm(nodes, w_node_in_ref[:width]) + mm(inbox, w_node_in_ref[width:])
    sigma = sigmoid(pre)
    zed = (pre * sigma).astype(BF16)
    unit, inv_std = normalize(mm(zed, w_node_out_ref[...]))
    upstream = cot_ref[...].astype(F32)
    dy = norm_back(upstream, unit, inv_std).astype(BF16)
    db = (mm_cols(dy, w_node_out_ref[...]) * (sigma * (1.0 + pre * (1.0 - sigma)))).astype(BF16)
    dagg_ref[...] = mm_cols(db, w_node_in_ref[width:]).astype(BF16)
    node_part_ref[...] = upstream + mm_cols(db, w_node_in_ref[:width])
    grads_no[...] = mm_rows(zed, dy)
    grads_ni[:width] = mm_rows(nodes, db)
    grads_ni[width:] = mm_rows(inbox, db)
    put_blocks((grads_no, grads_ni), lax.axis_index("patch"), count, keep_ref, away_ref)


def backward_kernel(
    first, recv_ref, zeta_ref, slope_ref, normed_ref, inv_ref, dagg_ref, w_edge_out_ref, dye_ref, da_ref
):
    rows = slice(first, first + dye_ref.shape[0])
    up = mm(one_hot_cols(recv_ref[:, rows], dagg_ref.shape[0]), dagg_ref[...])
    dye = norm_back(up, normed_ref[rows].astype(F32), inv_ref[rows]).astype(BF16)
    dye_ref[...] = dye
    da_ref[...] = (mm_cols(dye, w_edge_out_ref[...]) * slope_ref[rows].astype(F32)).astype(BF16)


def weights_kernel(
    count,
    slot,
    halo_ref,
    send_ref,
    recv_ref,
    nodes_ref,
    edges1_ref,
    edges2_ref,
    zeta_ref,
    dye1_ref,
    dye2_ref,
    da1_ref,
    da2_ref,
    keep_ref,
    away1_ref,
    away2_ref,
    away3_ref,
    away4_ref,
    own_ref,
    recv_sums_ref,
    far_ref,
    sums,
    grads_eo,
    grads_ei,
):
    owned, width = nodes_ref.shape
    n_table = sums.shape[0]
    n_far = count * slot
    me = lax.axis_index("patch")

    def block_of(device):
        return cube_place(device ^ me, device & 1, count) * slot

    half = da1_ref.shape[0]
    sender, safe, _ = edge_ids(slice(None), owned, slot, send_ref, recv_ref, block_of)
    hot = hot_rows(sender, safe, n_table)
    sums[...] = mm(hot[:, :half], da1_ref[...]) + mm(hot[:, half:], da2_ref[...])

    own = sums[:owned].astype(BF16)
    recv = sums[owned : 2 * owned].astype(BF16)
    far = sums[2 * owned : 2 * owned + n_far].astype(BF16)
    own_ref[...] = own
    recv_sums_ref[...] = recv
    far_ref[...] = far
    away4_ref[away3_ref.shape[0] :] = far[n_far // 2 :]
    shape = (n_far, count * HALO_ROWS)
    column = lax.broadcasted_iota(jnp.int32, shape, 1)
    device = column // HALO_ROWS
    there = (column % HALO_ROWS < slot) & (
        block_of(device) + column % HALO_ROWS == lax.broadcasted_iota(jnp.int32, shape, 0)
    )
    halo = mm(jnp.where(there, 1.0, 0.0).astype(BF16), halo_ref[...]).astype(BF16)
    nodes = nodes_ref[...]
    for start in range(0, width, TILE):
        cols = slice(start, start + TILE)
        grads_eo[cols] = mm_rows(zeta_ref[:half, cols], dye1_ref[...]) + mm_rows(zeta_ref[half:, cols], dye2_ref[...])
        grads_ei[cols] = mm_rows(edges1_ref[:, cols], da1_ref[...]) + mm_rows(edges2_ref[:, cols], da2_ref[...])
    grads_ei[width : 2 * width] = mm_rows(nodes, own) + mm_rows(halo, far)
    grads_ei[2 * width :] = mm_rows(nodes, recv)
    put_blocks((grads_eo, grads_ei), me, count, keep_ref, away1_ref, away2_ref, away3_ref, away4_ref)


def move_rows(step, count, slot):
    take = take_rows(step, count, slot)
    rows = take.shape[1]
    square = lax.broadcasted_iota(jnp.int32, (rows, rows), 0) == lax.broadcasted_iota(jnp.int32, (rows, rows), 1)
    eye = jnp.where(square, 1.0, 0.0)
    stay = (eye - mm_rows(take, take)).astype(BF16)
    small = eye[: rows // 2, : rows // 2].astype(BF16)
    after = jnp.concatenate([stay, mm_rows(take, small).astype(BF16)], axis=1)
    return jnp.concatenate([mm(take_rows(step + 1, count, slot), after).astype(BF16), after], axis=0)


def ride_kernel(step, pieces, keep_ref, far_ref, *refs):
    arrived_refs, (moves_ref, next_keep_ref, next_away_ref, next_far_ref) = refs[:pieces], refs[pieces:]
    size, half = keep_ref.shape[0], next_keep_ref.shape[0]
    each = size // pieces
    moved = mm(moves_ref[step], jnp.concatenate([far_ref[...], arrived_refs[-1][each:]], axis=0)).astype(BF16)
    for i, ref in enumerate(arrived_refs):
        start = i * each
        stop = start + each
        near = min(stop, half)
        if start < half:
            next_keep_ref[start:near] = keep_ref[start:near] + ref[: near - start]
        if stop > half:
            first = max(start, half)
            next_away_ref[first - half : stop - half] = keep_ref[first:stop] + ref[first - start : each]
    split = moved.shape[0] - next_far_ref.shape[0]
    next_away_ref[half:] = moved[:split]
    next_far_ref[...] = moved[split:]


def node_kernel(
    step, count, slot, own_ref, recv_ref, part_ref, w_send_ref, w_recv_ref, far_ref, pick_ref, out_ref, late_pick_ref
):
    take = take_rows(step, count, slot)
    stays = mm_rows(take, jnp.ones((take.shape[0], pick_ref.shape[1]), BF16)) == 0.0
    early_pick = jnp.where(stays, pick_ref[...], jnp.zeros_like(pick_ref[...]))
    late_pick_ref[...] = mm(take, pick_ref[...]).astype(BF16)
    own = own_ref[...].astype(F32) + mm_rows(early_pick, far_ref[...])
    out_ref[...] = (
        part_ref[...] + mm_cols(own.astype(BF16), w_send_ref[...]) + mm_cols(recv_ref[...], w_recv_ref[...])
    )


def last_kernel(keep_ref, arrived_ref, late_pick_ref, node_ref, w_send_ref, first_ref, rest_ref, grad_ref):
    share, rest = first_ref.shape[0], rest_ref.shape[0]
    size = keep_ref.shape[0]
    far = mm_cols(arrived_ref[size:], w_send_ref[...]).astype(BF16)
    total = keep_ref[...].astype(F32) + arrived_ref[:size].astype(F32)
    first_ref[...] = total[:share]
    rest_ref[...] = total[share : share + rest]
    grad_ref[...] = (node_ref[...] + mm_rows(late_pick_ref[...], far)).astype(BF16)


def add_kernel(keep_ref, arrived_ref, next_keep_ref, next_send_ref):
    half = next_keep_ref.shape[0]
    next_send_ref[...] = keep_ref[half:] + arrived_ref[half:]
    next_keep_ref[...] = keep_ref[:half] + arrived_ref[:half]


def total_kernel(kept_ref, came_ref, first_ref, rest_ref):
    share = first_ref.shape[0]
    total = kept_ref[...].astype(F32) + came_ref[...].astype(F32)
    first_ref[...] = total[:share]
    rest_ref[...] = total[share : share + rest_ref.shape[0]]


VMEM = pl.BlockSpec(memory_space=pltpu.VMEM)
HBM = pl.BlockSpec(memory_space=pltpu.HBM)
COST = pl.CostEstimate(flops=1 << 10, bytes_accessed=1 << 10, transcendentals=0)
LARGE_COST = pl.CostEstimate(flops=1 << 10, bytes_accessed=1 << 26, transcendentals=0)


def kernel_call(kernel, name, outs, scratch, args, near=(), far=(), limit=16, cost=COST, out_spec=None):
    specs = [VMEM] * (len(args) + len(near)) + [HBM] * len(far)
    near = [pltpu.with_memory_space_constraint(array, pltpu.VMEM) for array in near]
    far = [pltpu.with_memory_space_constraint(array, pltpu.HBM) for array in far]
    return pl.pallas_call(
        kernel,
        out_shape=tuple(outs),
        in_specs=specs,
        out_specs=(out_spec or VMEM,) * len(outs),
        scratch_shapes=scratch,
        compiler_params=pltpu.CompilerParams(vmem_limit_bytes=limit << 20),
        cost_estimate=cost,
        name=name,
    )(*args, *near, *far)


def in_order(first, then):
    return lax.optimization_barrier((first, then))


def trade(rows):
    return lax.all_to_all(rows, "patch", split_axis=0, concat_axis=0, tiled=True)


def body(
    count,
    nodes,
    edges,
    cot_nodes,
    w_edge_in,
    w_edge_out,
    w_node_in,
    w_node_out,
    send_rows,
    edge_sender,
    edge_receiver,
):
    owned, width = nodes.shape
    n_edges = edges.shape[0]
    slot = send_rows.shape[2]
    share = width // count
    n_halo = count * HALO_ROWS
    sender = edge_sender.reshape(1, -1)
    receiver = edge_receiver.reshape(1, -1)

    def space(*shape, dtype=BF16):
        return pltpu.VMEM(shape, dtype)

    def block_pair(rows, riders=0):
        size = count // 2 * (-(-(rows * share) // 16) * 16)
        return [space(size, width), space(size + riders, width)]

    n_far = count * slot
    steps = count.bit_length() - 1
    pick, halo_out = kernel_call(
        functools.partial(pick_kernel, count),
        "pick",
        [jax.ShapeDtypeStruct((n_far, owned), BF16), jax.ShapeDtypeStruct((n_halo, width), BF16)],
        [],
        (send_rows[0].T, nodes),
        limit=60,
    )
    halo = trade(halo_out)
    rows, square, ids = space(n_edges, width), space(width, width), space(1, n_edges, dtype=jnp.int32)
    half_rows = space(n_edges // 2, width)
    *near, moves = kernel_call(
        functools.partial(local_kernel, count, slot),
        "local",
        [space(owned, width), square, square, space(width + 2 * owned, width), half_rows]
        + [space(steps - 1, n_far * 3 // 2, n_far * 3 // 2)],
        [square, pltpu.SemaphoreType.DMA((6,))],
        (),
        far=(nodes, w_edge_in, w_edge_out, edges),
    )
    near_nodes, w_send, near_out, _, edges1 = near
    keep1, away1, zeta, slope, normed, inv, dagg, node_part, edges2, w_recv, sender, receiver = kernel_call(
        functools.partial(forward_kernel, count, slot),
        "forward",
        block_pair(3)
        + [rows, rows, rows, space(n_edges, 1, dtype=F32)]
        + [space(owned, width), space(owned, width, dtype=F32), half_rows, square, ids, ids],
        [space(2 * width, width), square, space(owned, width), space(width + 2 * owned + n_halo, width)]
        + [space(r, width, dtype=F32) for r in (owned, width, 2 * width)]
        + [pltpu.SemaphoreType.DMA((7,))],
        (halo,),
        near=near,
        far=(edges, sender, receiver, w_node_in, w_node_out, cot_nodes, w_edge_in),
        limit=36,
    )

    def add(keep, arrived):
        half = [space(keep.shape[0] // 2, width)] * 2
        return kernel_call(add_kernel, "add", half, [], (keep, arrived), limit=8, cost=LARGE_COST)

    def ride(step, keep, arrived, far):
        half = keep.shape[0] // 2
        outs = [space(half, width), space(half + n_far // 2, width), space(n_far, width)]
        kernel = functools.partial(ride_kernel, step, len(arrived))
        return kernel_call(kernel, "ride", outs, [], (keep, far, *arrived), (moves,), limit=8)

    came1 = cube_permute(away1, 0, count)
    halves = [half_rows] * 2
    args = (receiver, zeta, slope, normed, inv, dagg, near_out)
    dye1, da1 = kernel_call(functools.partial(backward_kernel, 0), "backward", halves, [], (), args)
    came1, dye1 = in_order(came1, dye1)
    keep1, away1 = add(keep1, came1)
    away1, dagg = in_order(away1, dagg)
    came1 = cube_permute(away1, 1, count)
    args = (receiver, zeta, slope, normed, inv, dagg, near_out)
    dye2, da2 = kernel_call(functools.partial(backward_kernel, n_edges // 2), "backward", halves, [], (), args)
    keep_shape = block_pair(4)[0]
    piece_shapes = [space(keep_shape.shape[0] // 4 + riders, width) for riders in (0, 0, 0, n_far // 2)]
    keep2, *pieces, own_sums, recv_sums, far_sums = kernel_call(
        functools.partial(weights_kernel, count, slot),
        "weights",
        [keep_shape, *piece_shapes, space(owned, width), space(owned, width), space(n_far, width)],
        [space(r, width, dtype=F32) for r in (2 * owned + -(-n_far // LANES) * LANES, width, 3 * width)],
        (halo,),
        (sender, receiver, near_nodes, edges1, edges2, zeta, dye1, dye2, da1, da2),
    )
    came2 = [cube_permute(piece, 0, count) for piece in pieces]
    for step in range(1, steps - 1):
        keep1, away1 = add(keep1, came1)
        away1, came2 = in_order(away1, came2)
        came1 = cube_permute(away1, step + 1, count)
        keep2, away2, far_sums = ride(step - 1, keep2, came2, far_sums)
        came2 = [cube_permute(away2, step, count)]
    keep2, away2, far_sums = ride(steps - 2, keep2, came2, far_sums)
    came1, away2 = in_order(came1, away2)
    _, (da1, da2, own_sums) = in_order(away2, (da1, da2, own_sums))
    came2 = cube_permute(away2, steps - 1, count)
    edge_grad = mm_cols(jnp.concatenate([da1, da2]), w_edge_in[:width]).astype(BF16)
    node_sum, late_pick = kernel_call(
        functools.partial(node_kernel, steps - 1, count, slot),
        "node",
        [space(owned, width, dtype=F32), space(n_far // 2, owned)],
        [],
        (own_sums, recv_sums, node_part, w_send, w_recv, far_sums, pick),
    )

    def whole(*parts):
        return [jax.ShapeDtypeStruct((part * share, width), F32) for part in parts]

    node_out, node_in = kernel_call(total_kernel, "node_total", whole(1, 2), [], (keep1, came1), limit=8)
    edge_out, edge_in, node_grad = kernel_call(
        last_kernel,
        "last",
        whole(1, 3) + [jax.ShapeDtypeStruct((owned, width), BF16)],
        [],
        (keep2, came2, late_pick, node_sum, w_send),
        limit=8,
    )
    return node_grad, edge_grad, edge_in, edge_out, node_in, node_out


def solution(mesh):
    rows = P(("groups", "patch"), None)
    flat = P(("groups", "patch"))
    return jax.shard_map(
        functools.partial(body, mesh.shape["patch"]),
        mesh=mesh,
        in_specs=(rows, rows, rows, P(), P(), P(), P(), P(("groups", "patch"), None, None), flat, flat),
        out_specs=(rows,) * 6,
        check_vma=False,
    )
```

```python
import functools

import jax
import jax.numpy as jnp
from jax import lax
from jax.experimental import pallas as pl
from jax.experimental.pallas import tpu as pltpu
from jax.sharding import PartitionSpec as P

BF16 = jnp.bfloat16
F32 = jnp.float32
EPS = 1e-05
LANES = 128
TILE = 256
HALO_ROWS = 8


def mm(left, right):
    return jnp.dot(left, right, preferred_element_type=F32)


def mm_rows(left, right):
    return lax.dot_general(left, right, (((0,), (0,)), ((), ())), preferred_element_type=F32)


def mm_cols(left, right):
    return lax.dot_general(left, right, (((1,), (1,)), ((), ())), preferred_element_type=F32)


def sigmoid(values):
    return 0.5 * jnp.tanh(0.5 * values) + 0.5


def normalize(values):
    center = values - jnp.mean(values, axis=-1, keepdims=True)
    inv_std = lax.rsqrt(jnp.mean(center * center, axis=-1, keepdims=True) + EPS)
    return center * inv_std, inv_std


def norm_back(upstream, normed, inv_std):
    return inv_std * (
        upstream
        - jnp.mean(upstream, axis=-1, keepdims=True)
        - normed * jnp.mean(upstream * normed, axis=-1, keepdims=True)
    )


def cube_masks(count):
    return [1 << i for i in range(count.bit_length() - 1)]


def cube_orders(count):
    rest = list(range(1, count.bit_length() - 1))
    return [0] + rest, [0] + rest[:2][::-1] + rest[2:]


def cube_place(apart, parity, count):
    bits = count.bit_length() - 1
    coords = [(apart >> i) & 1 for i in range(bits)]
    even, odd = [sum(coords[dim] << (bits - 1 - j) for j, dim in enumerate(order)) for order in cube_orders(count)]
    return jnp.where(parity == 0, even, odd)


def cube_permute(blocks, step, count):
    mask, orders = cube_masks(count), cube_orders(count)
    pairs = [(i, i ^ mask[orders[i & 1][step]]) for i in range(count)]
    return lax.ppermute(blocks, "patch", pairs)


def one_hot_cols(ids, width):
    rows = ids.shape[1]
    spread = jnp.transpose(jnp.broadcast_to(ids, (LANES, rows)))
    lane = lax.broadcasted_iota(jnp.int32, (rows, LANES), 1)
    tiles = [jnp.where(spread == lane + start, 1.0, 0.0).astype(BF16) for start in range(0, width, LANES)]
    return jnp.concatenate(tiles, axis=1)[:, :width]


def hot_cols(first, second, width):
    rows = first.shape[1]
    left = jnp.transpose(jnp.broadcast_to(first, (LANES, rows)))
    right = jnp.transpose(jnp.broadcast_to(second, (LANES, rows)))
    lane = lax.broadcasted_iota(jnp.int32, (rows, LANES), 1)
    tiles = [
        jnp.where((left == lane + start) | (right == lane + start), 1.0, 0.0).astype(BF16)
        for start in range(0, width, LANES)
    ]
    return jnp.concatenate(tiles, axis=1)


def hot_rows(first, second, width):
    row = lax.broadcasted_iota(jnp.int32, (width, first.shape[1]), 0)
    return jnp.where((row == first) | (row == second), 1.0, 0.0).astype(BF16)


def edge_ids(rows, owned, slot, send_ref, recv_ref, block_of):
    sender = send_ref[:, rows]
    receiver = recv_ref[:, rows]
    far = sender - owned
    sender = jnp.where(far < 0, sender, 2 * owned + block_of(far // slot) + far % slot)
    return sender, jnp.maximum(receiver, 0) + owned, receiver


def take_rows(step, count, slot):
    weight = count >> (step + 1)
    shape = (count // 2 * slot, count * slot)
    out = lax.broadcasted_iota(jnp.int32, shape, 0)
    block, row = out // slot, out % slot
    place = block // weight * 2 * weight + weight + block % weight
    return jnp.where(lax.broadcasted_iota(jnp.int32, shape, 1) == place * slot + row, 1.0, 0.0).astype(BF16)


def put_blocks(sources, me, count, keep_ref, *send_refs):
    shares = [source.shape[0] // count for source in sources]
    half = count // 2
    size = keep_ref.shape[0] // half
    spare = size - sum(shares)
    bits = count.bit_length() - 1
    for place in range(count):
        apart = [
            sum(((place >> (bits - 1 - j)) & 1) << dim for j, dim in enumerate(order)) for order in cube_orders(count)
        ]
        odd_target = (me ^ (place // half)) & 1
        target = me ^ jnp.where(odd_target == 0, *apart)
        parts = [
            source[pl.ds(pl.multiple_of(target * share, share), share)] for source, share in zip(sources, shares)
        ]
        if spare:
            parts.append(jnp.zeros((spare, keep_ref.shape[1]), F32))
        each = half // len(send_refs)
        ref = keep_ref if place < half else send_refs[(place - half) // each]
        start = (place if place < half else place % each) * size
        ref[start : start + size] = jnp.concatenate(parts, axis=0).astype(BF16)


def choose_rows(picks_ref, rows, owned, start):
    slot, count = picks_ref.shape
    shape = (rows, count)
    row = lax.broadcasted_iota(jnp.int32, shape, 0)
    first = start(lax.broadcasted_iota(jnp.int32, shape, 1))
    ids = jnp.zeros(shape, jnp.int32)
    for place in range(slot):
        ids = ids + jnp.where(row == first + place, picks_ref[place : place + 1] + 1, 0)
    ids = jnp.sum(ids.astype(F32), axis=1, keepdims=True).astype(jnp.int32) - 1
    node = lax.broadcasted_iota(jnp.int32, (rows, owned), 1)
    return jnp.where(node == ids, 1.0, 0.0).astype(BF16)


def pick_kernel(picks_ref, nodes_ref, rows_ref):
    chosen = choose_rows(picks_ref, rows_ref.shape[0], nodes_ref.shape[0], lambda device: device * HALO_ROWS)
    rows_ref[...] = mm(chosen, nodes_ref[...]).astype(BF16)


def local_kernel(
    count,
    slot,
    nodes_far,
    w_edge_in_far,
    w_edge_out_far,
    edges_far,
    nodes_ref,
    w_send,
    w_edge_out_ref,
    table,
    edges1_ref,
    moves_ref,
    w_recv,
    sems,
):
    owned, width = nodes_ref.shape
    pairs = (
        (nodes_far, nodes_ref),
        (w_edge_in_far.at[width : 2 * width], w_send),
        (w_edge_in_far.at[2 * width :], w_recv),
        (w_edge_in_far.at[:width], table.at[:width]),
        (w_edge_out_far, w_edge_out_ref),
        (edges_far.at[: edges1_ref.shape[0]], edges1_ref),
    )
    copies = [pltpu.make_async_copy(src, dst, sems.at[i]) for i, (src, dst) in enumerate(pairs)]
    for copy in copies:
        copy.start()
    for step in range(moves_ref.shape[0]):
        moves_ref[step] = move_rows(step, count, slot)
    copies[0].wait()
    nodes = nodes_ref[...]
    copies[1].wait()
    table[width : width + owned] = mm(nodes, w_send[...]).astype(BF16)
    copies[2].wait()
    table[width + owned :] = mm(nodes, w_recv[...]).astype(BF16)
    for copy in copies[3:]:
        copy.wait()


def forward_kernel(
    count,
    slot,
    halo_ref,
    nodes_ref,
    w_send,
    w_edge_out_ref,
    own_table,
    edges1_ref,
    edges_far,
    send_far,
    recv_far,
    w_node_in_far,
    w_node_out_far,
    cot_far,
    w_edge_in_far,
    keep_ref,
    away_ref,
    zeta_ref,
    slope_ref,
    normed_ref,
    inv_ref,
    dagg_ref,
    node_part_ref,
    edges2_ref,
    w_recv,
    send_ref,
    recv_ref,
    w_node_in_ref,
    w_node_out_ref,
    cot_ref,
    table,
    agg,
    grads_no,
    grads_ni,
    sems,
):
    owned, width = nodes_ref.shape
    n_table = table.shape[0]
    half = edges1_ref.shape[0]
    pairs = (
        (send_far, send_ref),
        (recv_far, recv_ref),
        (edges_far.at[half:], edges2_ref),
        (w_node_in_far, w_node_in_ref),
        (w_node_out_far, w_node_out_ref),
        (cot_far, cot_ref),
        (w_edge_in_far.at[2 * width :], w_recv),
    )
    copies = [pltpu.make_async_copy(src, dst, sems.at[i]) for i, (src, dst) in enumerate(pairs)]
    for copy in copies:
        copy.start()
    nodes = nodes_ref[...]
    table[: width + 2 * owned] = own_table[...]
    table[width + 2 * owned :] = mm(halo_ref[...], w_send[...]).astype(BF16)
    for copy in copies[:2]:
        copy.wait()
    for part, edges_ref in enumerate((edges1_ref, edges2_ref)):
        if part:
            copies[2].wait()
        rows = slice(part * half, (part + 1) * half)
        sender, safe, receiver = edge_ids(rows, owned, slot, send_ref, recv_ref, lambda device: device * HALO_ROWS)
        hot = hot_cols(sender, safe, n_table - width)
        pre = mm(jnp.concatenate([edges_ref[...], hot], axis=1), table[...])
        sigma = sigmoid(pre)
        zed = (pre * sigma).astype(BF16)
        zeta_ref[rows] = zed
        slope_ref[rows] = (sigma * (1.0 + pre * (1.0 - sigma))).astype(BF16)
        unit, inv_std = normalize(mm(zed, w_edge_out_ref[...]))
        message = unit.astype(BF16)
        normed_ref[rows] = message
        inv_ref[rows] = inv_std
        gathered = mm(hot_rows(receiver, receiver, owned), message)
        agg[...] = agg[...] + gathered if part else gathered

    for copy in copies[3:]:
        copy.wait()
    inbox = agg[...].astype(BF16)
    pre = mm(nodes, w_node_in_ref[:width]) + mm(inbox, w_node_in_ref[width:])
    sigma = sigmoid(pre)
    zed = (pre * sigma).astype(BF16)
    unit, inv_std = normalize(mm(zed, w_node_out_ref[...]))
    upstream = cot_ref[...].astype(F32)
    dy = norm_back(upstream, unit, inv_std).astype(BF16)
    db = (mm_cols(dy, w_node_out_ref[...]) * (sigma * (1.0 + pre * (1.0 - sigma)))).astype(BF16)
    dagg_ref[...] = mm_cols(db, w_node_in_ref[width:]).astype(BF16)
    node_part_ref[...] = upstream + mm_cols(db, w_node_in_ref[:width])
    grads_no[...] = mm_rows(zed, dy)
    grads_ni[:width] = mm_rows(nodes, db)
    grads_ni[width:] = mm_rows(inbox, db)
    put_blocks((grads_no, grads_ni), lax.axis_index("patch"), count, keep_ref, away_ref)


def backward_kernel(
    first, recv_ref, zeta_ref, slope_ref, normed_ref, inv_ref, dagg_ref, w_edge_out_ref, dye_ref, da_ref
):
    rows = slice(first, first + dye_ref.shape[0])
    up = mm(one_hot_cols(recv_ref[:, rows], dagg_ref.shape[0]), dagg_ref[...])
    dye = norm_back(up, normed_ref[rows].astype(F32), inv_ref[rows]).astype(BF16)
    dye_ref[...] = dye
    da_ref[...] = (mm_cols(dye, w_edge_out_ref[...]) * slope_ref[rows].astype(F32)).astype(BF16)


def weights_kernel(
    count,
    slot,
    halo_ref,
    send_ref,
    recv_ref,
    nodes_ref,
    edges1_ref,
    edges2_ref,
    zeta_ref,
    dye1_ref,
    dye2_ref,
    da1_ref,
    da2_ref,
    keep_ref,
    away1_ref,
    away2_ref,
    away3_ref,
    away4_ref,
    own_ref,
    recv_sums_ref,
    far_ref,
    sums,
    grads_eo,
    grads_ei,
):
    owned, width = nodes_ref.shape
    n_table = sums.shape[0]
    n_far = count * slot
    me = lax.axis_index("patch")

    def block_of(device):
        return cube_place(device ^ me, device & 1, count) * slot

    half = da1_ref.shape[0]
    sender, safe, _ = edge_ids(slice(None), owned, slot, send_ref, recv_ref, block_of)
    hot = hot_rows(sender, safe, n_table)
    sums[...] = mm(hot[:, :half], da1_ref[...]) + mm(hot[:, half:], da2_ref[...])

    own = sums[:owned].astype(BF16)
    recv = sums[owned : 2 * owned].astype(BF16)
    far = sums[2 * owned : 2 * owned + n_far].astype(BF16)
    own_ref[...] = own
    recv_sums_ref[...] = recv
    far_ref[...] = far
    away4_ref[away3_ref.shape[0] :] = far[n_far // 2 :]
    shape = (n_far, count * HALO_ROWS)
    column = lax.broadcasted_iota(jnp.int32, shape, 1)
    device = column // HALO_ROWS
    there = (column % HALO_ROWS < slot) & (
        block_of(device) + column % HALO_ROWS == lax.broadcasted_iota(jnp.int32, shape, 0)
    )
    halo = mm(jnp.where(there, 1.0, 0.0).astype(BF16), halo_ref[...]).astype(BF16)
    nodes = nodes_ref[...]
    for start in range(0, width, TILE):
        cols = slice(start, start + TILE)
        grads_eo[cols] = mm_rows(zeta_ref[:half, cols], dye1_ref[...]) + mm_rows(zeta_ref[half:, cols], dye2_ref[...])
        grads_ei[cols] = mm_rows(edges1_ref[:, cols], da1_ref[...]) + mm_rows(edges2_ref[:, cols], da2_ref[...])
    grads_ei[width : 2 * width] = mm_rows(nodes, own) + mm_rows(halo, far)
    grads_ei[2 * width :] = mm_rows(nodes, recv)
    put_blocks((grads_eo, grads_ei), me, count, keep_ref, away1_ref, away2_ref, away3_ref, away4_ref)


def move_rows(step, count, slot):
    take = take_rows(step, count, slot)
    rows = take.shape[1]
    square = lax.broadcasted_iota(jnp.int32, (rows, rows), 0) == lax.broadcasted_iota(jnp.int32, (rows, rows), 1)
    eye = jnp.where(square, 1.0, 0.0)
    stay = (eye - mm_rows(take, take)).astype(BF16)
    small = eye[: rows // 2, : rows // 2].astype(BF16)
    after = jnp.concatenate([stay, mm_rows(take, small).astype(BF16)], axis=1)
    return jnp.concatenate([mm(take_rows(step + 1, count, slot), after).astype(BF16), after], axis=0)


def ride_kernel(step, pieces, keep_ref, far_ref, *refs):
    arrived_refs, (moves_ref, next_keep_ref, next_away_ref, next_far_ref) = refs[:pieces], refs[pieces:]
    size, half = keep_ref.shape[0], next_keep_ref.shape[0]
    each = size // pieces
    moved = mm(moves_ref[step], jnp.concatenate([far_ref[...], arrived_refs[-1][each:]], axis=0)).astype(BF16)
    for i, ref in enumerate(arrived_refs):
        start = i * each
        stop = start + each
        near = min(stop, half)
        if start < half:
            next_keep_ref[start:near] = keep_ref[start:near] + ref[: near - start]
        if stop > half:
            first = max(start, half)
            next_away_ref[first - half : stop - half] = keep_ref[first:stop] + ref[first - start : each]
    split = moved.shape[0] - next_far_ref.shape[0]
    next_away_ref[half:] = moved[:split]
    next_far_ref[...] = moved[split:]


def node_kernel(
    step, count, slot, own_ref, recv_ref, part_ref, w_send_ref, w_recv_ref, far_ref, picks_ref, out_ref, late_pick_ref
):
    me = lax.axis_index("patch")
    take = take_rows(step, count, slot)
    pick = choose_rows(
        picks_ref, count * slot, own_ref.shape[0], lambda device: cube_place(device ^ me, me & 1, count) * slot
    )
    stays = mm_rows(take, jnp.ones((take.shape[0], pick.shape[1]), BF16)) == 0.0
    early_pick = jnp.where(stays, pick, jnp.zeros_like(pick))
    late_pick_ref[...] = mm(take, pick).astype(BF16)
    own = own_ref[...].astype(F32) + mm_rows(early_pick, far_ref[...])
    out_ref[...] = (
        part_ref[...] + mm_cols(own.astype(BF16), w_send_ref[...]) + mm_cols(recv_ref[...], w_recv_ref[...])
    )


def last_kernel(keep_ref, arrived_ref, late_pick_ref, node_ref, w_send_ref, first_ref, rest_ref, grad_ref):
    share, rest = first_ref.shape[0], rest_ref.shape[0]
    size = keep_ref.shape[0]
    far = mm_cols(arrived_ref[size:], w_send_ref[...]).astype(BF16)
    total = keep_ref[...].astype(F32) + arrived_ref[:size].astype(F32)
    first_ref[...] = total[:share]
    rest_ref[...] = total[share : share + rest]
    grad_ref[...] = (node_ref[...] + mm_rows(late_pick_ref[...], far)).astype(BF16)


def add_kernel(keep_ref, arrived_ref, next_keep_ref, next_send_ref):
    half = next_keep_ref.shape[0]
    next_send_ref[...] = keep_ref[half:] + arrived_ref[half:]
    next_keep_ref[...] = keep_ref[:half] + arrived_ref[:half]


def total_kernel(kept_ref, came_ref, first_ref, rest_ref):
    share = first_ref.shape[0]
    total = kept_ref[...].astype(F32) + came_ref[...].astype(F32)
    first_ref[...] = total[:share]
    rest_ref[...] = total[share : share + rest_ref.shape[0]]


VMEM = pl.BlockSpec(memory_space=pltpu.VMEM)
HBM = pl.BlockSpec(memory_space=pltpu.HBM)
COST = pl.CostEstimate(flops=1 << 10, bytes_accessed=1 << 10, transcendentals=0)
LARGE_COST = pl.CostEstimate(flops=1 << 10, bytes_accessed=1 << 26, transcendentals=0)


def kernel_call(kernel, name, outs, scratch, args, near=(), far=(), limit=16, cost=COST, out_spec=None):
    specs = [VMEM] * (len(args) + len(near)) + [HBM] * len(far)
    near = [pltpu.with_memory_space_constraint(array, pltpu.VMEM) for array in near]
    far = [pltpu.with_memory_space_constraint(array, pltpu.HBM) for array in far]
    return pl.pallas_call(
        kernel,
        out_shape=tuple(outs),
        in_specs=specs,
        out_specs=(out_spec or VMEM,) * len(outs),
        scratch_shapes=scratch,
        compiler_params=pltpu.CompilerParams(vmem_limit_bytes=limit << 20),
        cost_estimate=cost,
        name=name,
    )(*args, *near, *far)


def in_order(first, then):
    return lax.optimization_barrier((first, then))


def trade(rows):
    return lax.all_to_all(rows, "patch", split_axis=0, concat_axis=0, tiled=True)


def body(
    count,
    nodes,
    edges,
    cot_nodes,
    w_edge_in,
    w_edge_out,
    w_node_in,
    w_node_out,
    send_rows,
    edge_sender,
    edge_receiver,
):
    owned, width = nodes.shape
    n_edges = edges.shape[0]
    slot = send_rows.shape[2]
    share = width // count
    n_halo = count * HALO_ROWS
    sender = edge_sender.reshape(1, -1)
    receiver = edge_receiver.reshape(1, -1)

    def space(*shape, dtype=BF16):
        return pltpu.VMEM(shape, dtype)

    def block_pair(rows, riders=0):
        size = count // 2 * (-(-(rows * share) // 16) * 16)
        return [space(size, width), space(size + riders, width)]

    n_far = count * slot
    steps = count.bit_length() - 1
    picks = send_rows[0].T
    halo_out = kernel_call(
        pick_kernel, "pick", [jax.ShapeDtypeStruct((n_halo, width), BF16)], [], (picks, nodes), limit=60
    )[0]
    halo = trade(halo_out)
    rows, square, ids = space(n_edges, width), space(width, width), space(1, n_edges, dtype=jnp.int32)
    half_rows = space(n_edges // 2, width)
    *near, moves = kernel_call(
        functools.partial(local_kernel, count, slot),
        "local",
        [space(owned, width), square, square, space(width + 2 * owned, width), half_rows]
        + [space(steps - 1, n_far * 3 // 2, n_far * 3 // 2)],
        [square, pltpu.SemaphoreType.DMA((6,))],
        (),
        far=(nodes, w_edge_in, w_edge_out, edges),
    )
    near_nodes, w_send, near_out, _, edges1 = near
    keep1, away1, zeta, slope, normed, inv, dagg, node_part, edges2, w_recv, sender, receiver = kernel_call(
        functools.partial(forward_kernel, count, slot),
        "forward",
        block_pair(3)
        + [rows, rows, rows, space(n_edges, 1, dtype=F32)]
        + [space(owned, width), space(owned, width, dtype=F32), half_rows, square, ids, ids],
        [space(2 * width, width), square, space(owned, width), space(width + 2 * owned + n_halo, width)]
        + [space(r, width, dtype=F32) for r in (owned, width, 2 * width)]
        + [pltpu.SemaphoreType.DMA((7,))],
        (halo,),
        near=near,
        far=(edges, sender, receiver, w_node_in, w_node_out, cot_nodes, w_edge_in),
        limit=36,
    )

    def add(keep, arrived):
        half = [space(keep.shape[0] // 2, width)] * 2
        return kernel_call(add_kernel, "add", half, [], (keep, arrived), limit=8, cost=LARGE_COST)

    def ride(step, keep, arrived, far):
        half = keep.shape[0] // 2
        outs = [space(half, width), space(half + n_far // 2, width), space(n_far, width)]
        kernel = functools.partial(ride_kernel, step, len(arrived))
        return kernel_call(kernel, "ride", outs, [], (keep, far, *arrived), (moves,), limit=8)

    came1 = cube_permute(away1, 0, count)
    halves = [half_rows] * 2
    args = (receiver, zeta, slope, normed, inv, dagg, near_out)
    dye1, da1 = kernel_call(functools.partial(backward_kernel, 0), "backward", halves, [], (), args)
    came1, dye1 = in_order(came1, dye1)
    keep1, away1 = add(keep1, came1)
    away1, dagg = in_order(away1, dagg)
    came1 = cube_permute(away1, 1, count)
    args = (receiver, zeta, slope, normed, inv, dagg, near_out)
    dye2, da2 = kernel_call(functools.partial(backward_kernel, n_edges // 2), "backward", halves, [], (), args)
    keep_shape = block_pair(4)[0]
    piece_shapes = [space(keep_shape.shape[0] // 4 + riders, width) for riders in (0, 0, 0, n_far // 2)]
    keep2, *pieces, own_sums, recv_sums, far_sums = kernel_call(
        functools.partial(weights_kernel, count, slot),
        "weights",
        [keep_shape, *piece_shapes, space(owned, width), space(owned, width), space(n_far, width)],
        [space(r, width, dtype=F32) for r in (2 * owned + -(-n_far // LANES) * LANES, width, 3 * width)],
        (halo,),
        (sender, receiver, near_nodes, edges1, edges2, zeta, dye1, dye2, da1, da2),
    )
    came2 = [cube_permute(piece, 0, count) for piece in pieces]
    for step in range(1, steps - 1):
        keep1, away1 = add(keep1, came1)
        away1, came2 = in_order(away1, came2)
        came1 = cube_permute(away1, step + 1, count)
        keep2, away2, far_sums = ride(step - 1, keep2, came2, far_sums)
        came2 = [cube_permute(away2, step, count)]
    keep2, away2, far_sums = ride(steps - 2, keep2, came2, far_sums)
    came1, away2 = in_order(came1, away2)
    _, (da1, da2, own_sums) = in_order(away2, (da1, da2, own_sums))
    came2 = cube_permute(away2, steps - 1, count)
    edge_grad = mm_cols(jnp.concatenate([da1, da2]), w_edge_in[:width]).astype(BF16)
    node_sum, late_pick = kernel_call(
        functools.partial(node_kernel, steps - 1, count, slot),
        "node",
        [space(owned, width, dtype=F32), space(n_far // 2, owned)],
        [],
        (own_sums, recv_sums, node_part, w_send, w_recv, far_sums, picks),
    )

    def whole(*parts):
        return [jax.ShapeDtypeStruct((part * share, width), F32) for part in parts]

    node_out, node_in = kernel_call(total_kernel, "node_total", whole(1, 2), [], (keep1, came1), limit=8)
    edge_out, edge_in, node_grad = kernel_call(
        last_kernel,
        "last",
        whole(1, 3) + [jax.ShapeDtypeStruct((owned, width), BF16)],
        [],
        (keep2, came2, late_pick, node_sum, w_send),
        limit=8,
    )
    return node_grad, edge_grad, edge_in, edge_out, node_in, node_out


def solution(mesh):
    rows = P(("groups", "patch"), None)
    flat = P(("groups", "patch"))
    return jax.shard_map(
        functools.partial(body, mesh.shape["patch"]),
        mesh=mesh,
        in_specs=(rows, rows, rows, P(), P(), P(), P(), P(("groups", "patch"), None, None), flat, flat),
        out_specs=(rows,) * 6,
        check_vma=False,
    )
```
